512 devices in a mesh: row: 16 (over y, core), col: 32 (over z, x).
Axes of the slice: x: 4, y: 8, z: 8, core: 2. Of those that a mesh axis runs over, the one named last changes fastest.
Arguments:
- matrix: bfloat16 [8192, 57344], P('row', 'col'), may hold values from -6 to 6
- lower_inv: float32 [2, 256, 256], replicated, may hold values from -1 to 1, as said below
- upper_inv: float32 [2, 256, 256], replicated, may hold values from -0.12 to 0.12, as said below
Outputs:
- factored: bfloat16 [8192, 57344], P('row', 'col')
The draws below stay inside these ranges and needn't reach their ends.
Inputs may be any that keep to these rules, and one draw needn't show every extreme that they name: `lower_inv`: ones on the diagonal and zeros above it. `upper_inv`: zeros below the diagonal; the diagonal is positive.
All inputs are finite; a program needn't handle non-finite values.
Results may differ from the reference program's by a relative error of at most 0.0069.
Values may be sent and summed in bfloat16 or wider, within the bound.
A program may use at most 64 MiB of HBM per device.

```python
import math
import jax
import jax.numpy as jnp
from jax import lax

NB = 256
RB_DEV = 2
CB_DEV = 7
ROWS = 8192
COLS = 57344
N_ROW = 16
N_COL = 32


def draw_lower_inv(key, part):
    key = jax.random.fold_in(key, 11)
    spread = jnp.clip(jax.random.normal(key, (2, NB, NB), jnp.float32), -4.0, 4.0)
    strict = jnp.tril(jnp.ones((NB, NB), jnp.float32), -1)
    return spread * strict * (0.5 / math.sqrt(NB)) + jnp.eye(NB, dtype=jnp.float32)


def draw_upper_inv(key, part):
    key = jax.random.fold_in(key, 23)
    first, second = jax.random.split(key)
    spread = jnp.clip(jax.random.normal(first, (2, NB, NB), jnp.float32), -4.0, 4.0)
    strict = jnp.triu(jnp.ones((NB, NB), jnp.float32), 1)
    diagonal = jnp.exp(jax.random.uniform(second, (2, NB), jnp.float32, math.log(0.04), math.log(0.12)))
    eye_table = jnp.eye(NB, dtype=jnp.float32)
    return spread * strict * (0.04 / math.sqrt(NB)) + diagonal[:, :, None] * eye_table[None, :, :]


def levels(key, dims, pieces, smallest, high):
    loudness, own = 1.0, jax.random.fold_in(key, 6)
    for dim, shards_of in pieces:
        heights = jnp.exp(jax.random.uniform(jax.random.fold_in(own, dim), (shards_of,), jnp.float32, smallest / len(pieces), high / len(pieces)))
        loudness = loudness * jnp.repeat(heights, dims[dim] // shards_of).reshape([-1 if axis == dim else 1 for axis in range(len(dims))])
    return loudness


def normal_values(key, shape, deviation, reach, pieces=(), held_as=jnp.bfloat16):
    level = levels(key, shape, pieces, -0.22, 0.18) if pieces else 1.0
    array = jax.random.normal(key, shape, jnp.float32) * deviation * level
    return jnp.minimum(jnp.maximum(array, -reach), reach).astype(held_as)


def setup_inputs(seed: int = 0) -> dict:
    seeds = jax.random.split(jax.random.key(seed), 4)
    return {
        "matrix": normal_values(seeds[0], (ROWS, COLS), 1.0, 6.0, ((0, 16), (1, 32))),
        "lower_inv": draw_lower_inv(jax.random.fold_in(seeds[3], 71), 0),
        "upper_inv": draw_upper_inv(jax.random.fold_in(seeds[3], 71), 0),
    }


def reference(matrix, lower_inv, upper_inv):
    width = NB
    rows_dev = RB_DEV * NB
    cols_dev = CB_DEV * NB
    stored_rows = jnp.arange(ROWS, dtype=jnp.int32)
    row_block = ((stored_rows % rows_dev) // width) * N_ROW + stored_rows // rows_dev
    stored_cols = jnp.arange(COLS, dtype=jnp.int32)
    col_block = ((stored_cols % cols_dev) // width) * N_COL + stored_cols // cols_dev

    def panel_pair(column, top_rows, section):
        lower = jnp.dot(column, upper_inv[section], precision=lax.Precision.HIGHEST, preferred_element_type=jnp.float32)
        lower = jnp.where((row_block > section)[:, None], lower, 0.0).astype(jnp.bfloat16)
        upper = jnp.dot(lower_inv[section], top_rows, precision=lax.Precision.HIGHEST, preferred_element_type=jnp.float32)
        upper = jnp.where((col_block > section)[None, :], upper, 0.0).astype(jnp.bfloat16)
        return lower, upper

    first_lower, first_upper = panel_pair(matrix[:, 0:width].astype(jnp.float32), matrix[0:width, :].astype(jnp.float32), 0)
    second_col = matrix[:, cols_dev:cols_dev + width].astype(jnp.float32) - jnp.dot(first_lower, first_upper[:, cols_dev:cols_dev + width], preferred_element_type=jnp.float32)
    second_top = matrix[rows_dev:rows_dev + width, :].astype(jnp.float32) - jnp.dot(first_lower[rows_dev:rows_dev + width], first_upper, preferred_element_type=jnp.float32)
    second_lower, second_upper = panel_pair(second_col, second_top, 1)
    lowers = jnp.concatenate([first_lower, second_lower], axis=1)
    uppers = jnp.concatenate([first_upper, second_upper], axis=0)
    panel_lowers = [first_lower, second_lower]

    grouped = matrix.reshape(ROWS, N_COL, cols_dev).transpose(1, 0, 2)
    upper_groups = uppers.reshape(2 * width, N_COL, cols_dev).transpose(1, 0, 2)
    col_groups = col_block.reshape(N_COL, cols_dev)

    def one_group(inputs):
        block, upper_block, blocks_here, group = inputs
        updated = block.astype(jnp.float32) - jnp.dot(lowers, upper_block, preferred_element_type=jnp.float32)
        for section in range(2):
            left = jnp.where((group == section) & (row_block > section)[:, None], panel_lowers[section].astype(jnp.float32), updated[:, 0:width])
            updated = updated.at[:, 0:width].set(left)
            start = section * rows_dev
            top_rows = updated[start:start + width]
            top_rows = jnp.where((blocks_here > section)[None, :], upper_block[section * width:(section + 1) * width].astype(jnp.float32), top_rows)
            updated = updated.at[start:start + width].set(top_rows)
        return updated.astype(jnp.bfloat16)

    result = lax.map(one_group, (grouped, upper_groups, col_groups, jnp.arange(N_COL, dtype=jnp.int32)))
    return result.transpose(1, 0, 2).reshape(ROWS, COLS)
```

```python
import functools

import jax
import jax.numpy as jnp
from jax import lax
from jax.experimental import pallas as pl
from jax.experimental.pallas import tpu as pltpu
from jax.sharding import PartitionSpec as P

MESH = pl.DeviceIdType.MESH
F32 = jnp.float32
BF16 = jnp.bfloat16
NB = 256
NY, NZ, NX = 8, 8, 4
HOP = 8

BOTH = {0: (2, 6), 2: (1, 3), 3: (4,), 6: (7, 5)}
CHAIN = {k: (k + 1,) for k in range(7)}
SKIP = {0: (2,), 2: (4, 1), 4: (6, 3), 6: (7, 5)}


def depths(tree):
    depth = {0: 0}
    todo = [0]
    while todo:
        k = todo.pop()
        for child in tree.get(k, ()):
            far = min((child - k) % 8, (k - child) % 8)
            depth[child] = depth[k] + HOP + (far - 1)
            todo.append(child)
    return [depth[k] for k in range(8)]


def offsets(tree, slot):
    out = []
    for k in range(8):
        children = tree.get(k, ())
        out.append((children[slot] - k + 4) % 8 - 4 if slot < len(children) else 0)
    return out


def lut(index, values):
    result = jnp.int32(values[0])
    for k in range(1, len(values)):
        if values[k] != values[0]:
            result = jnp.where(index == k, jnp.int32(values[k]), result)
    return result


GROUPS = ((BOTH, 4, 2), (CHAIN, 24, 1))
UCH = 28
LROWS = 64
LCH = 512 // LROWS
XCH = NB // LROWS


def split(value):
    high = value.astype(BF16)
    return high, (value - high.astype(F32)).astype(BF16)


def dot(a, b):
    return jnp.dot(a, b, preferred_element_type=F32)


def kernel(mat, linv, uinv, out, U, X, L, M, inv, LF, UF, work, l10, u01, us, ur, ps, pr, ls, lr, xs, xr, xp, xq, loc):
    r = lax.axis_index("row")
    c = lax.axis_index("col")
    y, core = r // 2, lax.rem(r, 2)
    z, x = c // NX, lax.rem(c, NX)
    sign = 1 - 2 * core
    p = lax.rem(NY + sign * y, NY)
    partner = (y * 2 + 1 - core, c)

    def at_y(off):
        return (lax.rem(y + off + NY, NY) * 2 + core, c)

    def at_z(off):
        return (r, lax.rem(z + off + NZ, NZ) * NX + x)

    def at_x(off):
        return (r, z * NX + lax.rem(x + off + NX, NX))

    barrier = pltpu.get_barrier_semaphore()
    near = [at_y(1), at_y(-1), at_y(2), at_y(-2), at_z(1), at_z(-1), at_z(2), at_z(-2), at_x(1), at_x(-1), partner]
    for device in near:
        pl.semaphore_signal(barrier, inc=1, device_id=device, device_id_type=MESH)

    local = [
        pltpu.make_async_copy(mat, M, loc.at[0]),
        pltpu.make_async_copy(linv, inv.at[0], loc.at[1]),
        pltpu.make_async_copy(uinv, inv.at[1], loc.at[2]),
    ]
    for copy in local:
        copy.start()
    own_rows = pltpu.make_async_copy(mat.at[pl.ds(0, NB)], U.at[core], loc.at[3])
    own_cols = pltpu.make_async_copy(mat.at[:, pl.ds(0, NB)], L.at[lax.rem(x, 2)], loc.at[4])
    src_u = p == 0
    src_l = c < 2

    @pl.when(src_u)
    def _():
        own_rows.start()

    @pl.when(src_l)
    def _():
        own_cols.start()

    pl.semaphore_wait(barrier, len(near))

    def remote(src, dst, send, recv, device):
        return pltpu.make_async_remote_copy(
            src_ref=src, dst_ref=dst, send_sem=send, recv_sem=recv, device_id=device, device_id_type=MESH
        )

    streams = []

    first, base = 0, 0
    u_lag0 = None
    for tree, count, stride in GROUPS:

        def u_part(ref, j, first=first):
            j = j + first
            col = pl.multiple_of(j // 2 * 128, 128)
            row = pl.multiple_of(lax.rem(j, 2) * 128, 128)
            return ref.at[pl.ds(row, 128), pl.ds(col, 128)]

        lag = base + lut(p, depths(tree))
        if u_lag0 is None:
            u_lag0 = lag
        children = []
        for slot in range(2):
            offs = offsets(tree, slot)
            if any(offs):
                off = lut(p, offs)
                children.append((off != 0, at_y(sign * off), lambda j, s=slot, f=first: (us.at[s, f + j], ur.at[f + j])))
        children.append((None, partner, lambda j, f=first: (ps.at[f + j], pr.at[f + j])))
        streams.append(
            dict(
                n=count,
                stride=stride,
                lag=lag,
                is_src=src_u,
                src=lambda j, part=u_part: part(mat, j),
                buf=lambda j, part=u_part: part(U.at[core], j),
                recv=lambda j, f=first: ur.at[f + j],
                children=children,
            )
        )
        first += count
        base += count * stride

    def plane(block):
        xr_ = lax.rem(x, NX) if block == 0 else lax.rem(1 - x + NX, NX)
        xs_ = 1 if block == 0 else -1
        lag = lut(z, depths(BOTH)) + lut(xr_, (0, HOP, 2 * HOP, HOP))
        children = []
        for slot in range(2):
            off = lut(z, offsets(BOTH, slot))
            children.append(((xr_ == 0) & (off != 0), at_z(off)))
        children.append((xr_ == 0, at_x(xs_)))
        off = lut(xr_, (-1, 0, 0, -1))
        children.append((off != 0, at_x(xs_ * off)))
        return lag, children, (xr_ == 0) & (z == 0)

    for block in range(2):
        lag, kids, is_src = plane(block)

        def l_part(ref, j):
            return ref.at[pl.ds(pl.multiple_of(j * LROWS, LROWS), LROWS), pl.ds(0, NB)]

        streams.append(
            dict(
                n=LCH,
                stride=2,
                lag=lag + block,
                is_src=is_src,
                src=lambda j: l_part(mat, j),
                buf=lambda j, b=block: l_part(L.at[b], j),
                recv=lambda j, b=block: lr.at[b, j],
                children=[
                    (cond, dev, lambda j, s=s, b=block: (ls.at[b, s, j], lr.at[b, j])) for s, (cond, dev) in enumerate(kids)
                ],
            )
        )

        mine = core == 1 - block
        x_lag = jnp.maximum(u_lag0 + 9, 2 * LCH) + lag
        streams.append(
            dict(
                n=XCH,
                stride=2,
                lag=x_lag,
                only=mine,
                is_src=is_src,
                src=lambda j: l_part(U.at[core], j),
                buf=lambda j: l_part(X.at[core], j),
                recv=lambda j: xr.at[j],
                children=[
                    (cond, dev, lambda j, s=s: (xs.at[s, j], xr.at[j])) for s, (cond, dev) in enumerate(kids)
                ]
                + [(None, partner, lambda j: (xp.at[j], xq.at[j]))],
            )
        )

    def when(cond, fn):
        if cond is None:
            fn()
        else:
            pl.when(cond)(fn)

    def handle(s, i):
        t = i - s["lag"]
        ok = (t >= 0) & (t < s["n"] * s["stride"])
        if s["stride"] > 1:
            ok = ok & (lax.rem(t, s["stride"]) == 0)
        if s.get("only") is not None:
            ok = ok & s["only"]

        @pl.when(ok)
        def _():
            j = t // s["stride"]

            def send(src):
                for cond, dev, sems in s["children"]:
                    a, b = sems(j)
                    when(cond, remote(src, s["buf"](j), a, b, dev).start)

            @pl.when(s["is_src"])
            def _():
                send(s["src"](j))

            @pl.when(jnp.logical_not(s["is_src"]))
            def _():
                buf = s["buf"](j)
                remote(buf, buf, s["recv"](j), s["recv"](j), partner).wait_recv()
                send(buf)

    steps = 160

    @pl.loop(0, steps)
    def _(i):
        @pl.when((i == 8) & src_u)
        def _():
            own_rows.wait()

        for s in streams:
            handle(s, i)

    @pl.when(src_l)
    def _():
        own_cols.wait()

    corner_src = src_l & (c == 1 - core)
    corner = pltpu.make_async_copy(U.at[core, :, pl.ds(0, NB)], X.at[core], loc.at[5])

    @pl.when(corner_src)
    def _():
        corner.start()
        corner.wait()

    @pl.loop(0, UCH)
    def _(j):
        col = pl.multiple_of(j // 2 * 128, 128)
        row = pl.multiple_of(lax.rem(j, 2) * 128, 128)
        buf = U.at[1 - core, pl.ds(row, 128), pl.ds(col, 128)]
        remote(buf, buf, pr.at[j], pr.at[j], partner).wait_recv()

    @pl.loop(0, XCH)
    def _(j):
        buf = X.at[1 - core, pl.ds(pl.multiple_of(j * LROWS, LROWS), LROWS)]
        remote(buf, buf, xq.at[j], xq.at[j], partner).wait_recv()

    for copy in local:
        copy.wait()

    li0h, li0l = split(inv[0, 0])
    li1h, li1l = split(inv[0, 1])
    ui0h, ui0l = split(inv[1, 0])
    ui1h, ui1l = split(inv[1, 1])
    for k, value in enumerate((li0h, li0l, li1h, li1l)):
        work[k] = value
    l10[...] = (dot(X[1], ui0h) + dot(X[1], ui0l)).astype(BF16)
    u01[...] = (dot(li0h, X[0]) + dot(li0l, X[0])).astype(BF16)
    for half in range(2):
        rows = pl.ds(half * NB, NB)
        block = half * 16 + r
        lower0 = dot(L[0, rows], ui0h) + dot(L[0, rows], ui0l)
        lower0 = jnp.where(block > 0, lower0, 0.0).astype(BF16)
        LF[rows, 0:NB] = lower0
        column = L[1, rows].astype(F32) - dot(lower0, u01[...])
        ch, cl = split(column)
        lower1 = dot(ch, ui1h) + dot(cl, ui1h) + dot(ch, ui1l)
        LF[rows, NB : 2 * NB] = jnp.where(block > 1, lower1, 0.0).astype(BF16)

    @pl.loop(0, 7)
    def _(q):
        cols = pl.ds(pl.multiple_of(q * NB, NB), NB)
        block = q * 32 + c
        upper0 = dot(work[0], U[0, :, cols]) + dot(work[1], U[0, :, cols])
        upper0 = jnp.where(block > 0, upper0, 0.0).astype(BF16)
        top = U[1, :, cols].astype(F32) - dot(l10[...], upper0)
        th, tl = split(top)
        upper1 = dot(work[2], th) + dot(work[3], th) + dot(work[2], tl)
        upper1 = jnp.where(block > 1, upper1, 0.0).astype(BF16)
        UF[0:NB] = upper0
        UF[NB : 2 * NB] = upper1
        out[:, cols] = (M[:, cols].astype(F32) - dot(LF[...], UF[...])).astype(BF16)

        @pl.when((r == 0) & (block > 0))
        def _():
            out[0:NB, cols] = UF[0:NB]

        @pl.when((r == 1) & (block > 1))
        def _():
            out[0:NB, cols] = UF[NB : 2 * NB]

    @pl.when((c == 0) & (r > 0))
    def _():
        out[0:NB, 0:NB] = LF[0:NB, 0:NB]

    @pl.when(c == 0)
    def _():
        out[NB : 2 * NB, 0:NB] = LF[NB : 2 * NB, 0:NB]

    @pl.when((c == 1) & (r > 1))
    def _():
        out[0:NB, 0:NB] = LF[0:NB, NB : 2 * NB]

    @pl.when(c == 1)
    def _():
        out[NB : 2 * NB, 0:NB] = LF[NB : 2 * NB, NB : 2 * NB]

    for s in streams:

        def drain(s=s):
            @pl.loop(0, s["n"])
            def _(j):
                for cond, dev, sems in s["children"]:
                    a, b = sems(j)
                    when(cond, remote(s["buf"](j), s["buf"](j), a, b, dev).wait_send)

        when(s.get("only"), drain)


def body(matrix, lower_inv, upper_inv):
    D = pltpu.SemaphoreType.DMA
    return pl.pallas_call(
        kernel,
        out_shape=jax.ShapeDtypeStruct(matrix.shape, matrix.dtype),
        in_specs=[pl.BlockSpec(memory_space=pl.ANY)] * 3,
        out_specs=pl.BlockSpec(memory_space=pltpu.VMEM),
        scratch_shapes=[
            pltpu.VMEM((2, NB, 1792), BF16),
            pltpu.VMEM((2, NB, NB), BF16),
            pltpu.VMEM((2, 512, NB), BF16),
            pltpu.VMEM((512, 1792), BF16),
            pltpu.VMEM((2, 2, NB, NB), F32),
            pltpu.VMEM((512, 512), BF16),
            pltpu.VMEM((512, NB), BF16),
            pltpu.VMEM((4, NB, NB), BF16),
            pltpu.VMEM((NB, NB), BF16),
            pltpu.VMEM((NB, NB), BF16),
            D((2, UCH)),
            D((UCH,)),
            D((UCH,)),
            D((UCH,)),
            D((2, 4, LCH)),
            D((2, LCH)),
            D((4, XCH)),
            D((XCH,)),
            D((XCH,)),
            D((XCH,)),
            D((6,)),
        ],
        compiler_params=pltpu.CompilerParams(
            collective_id=0, has_side_effects=True, vmem_limit_bytes=60 * 2**20
        ),
    )(matrix, lower_inv, upper_inv)


def solution(mesh):
    in_specs = (P("row", "col"), P(), P())
    return jax.shard_map(body, mesh=mesh, in_specs=in_specs, out_specs=P("row", "col"), check_vma=False)
```

```python
import jax
import jax.numpy as jnp
from jax import lax
from jax.experimental import pallas as pl
from jax.experimental.pallas import tpu as pltpu
from jax.sharding import PartitionSpec as P

MESH = pl.DeviceIdType.MESH
F32 = jnp.float32
BF16 = jnp.bfloat16
NB = 256
COLS = 1792
NY, NZ, NX = 8, 8, 4

NEAR = {0: (1, 7), 1: (2,), 2: (3,), 3: (4,), 7: (6,), 6: (5,)}
FAR = {0: (2, 6), 2: (1, 3), 3: (4,), 6: (7, 5)}
WIDE = {0: (2, 6), 2: (4, 3, 1), 6: (5, 7)}
LONG = {0: (2,), 2: (3, 1), 3: (4,), 4: (5,), 5: (6,), 6: (7,)}

GROUPS = (
    (WIDE, 0, 4, 0, 1, (0, 9, 5, 9, 10, 8, 5, 8)),
    (LONG, 4, 16, 4, 2, (-4, 9, 5, 9, 13, 17, 21, 25)),
    (NEAR, 20, 8, 12, 1, (-2, 5, 8, 12, 16, 12, 8, 5)),
)
UCH = 28
LROWS = 64
LCH = 512 // LROWS
XCH = NB // LROWS
STEPS = 42
PLANE = (2, 9, 6, 9, 14, 9, 6, 9)
PLANE_X = (0, 9, 5, 9, 10, 8, 5, 8)


def offsets(tree, slot):
    out = []
    for k in range(8):
        children = tree.get(k, ())
        out.append((children[slot] - k + 4) % 8 - 4 if slot < len(children) else 0)
    return out


def lut(index, values):
    result = jnp.int32(values[0])
    for k in range(1, len(values)):
        if values[k] != values[0]:
            result = jnp.where(index == k, jnp.int32(values[k]), result)
    return result


def split(value):
    high = value.astype(BF16)
    return high, (value - high.astype(F32)).astype(BF16)


def dot(a, b):
    return jnp.dot(a, b, preferred_element_type=F32)


def remote(src, dst, send, recv, device):
    return pltpu.make_async_remote_copy(
        src_ref=src, dst_ref=dst, send_sem=send, recv_sem=recv, device_id=device, device_id_type=MESH
    )


def gather(mat, linv, uinv, UF, LF, M, U, X, L, inv, W, small, D1, us, ur, ps, pr, ls, lr, xs, xr, xp, xq, ready, loc):
    r = lax.axis_index("row")
    c = lax.axis_index("col")
    y, core = r // 2, lax.rem(r, 2)
    z, x = c // NX, lax.rem(c, NX)
    sign = 1 - 2 * core
    p = lax.rem(NY + sign * y, NY)
    partner = (y * 2 + 1 - core, c)
    hub = x < 2
    fb = jnp.where((x == 1) | (x == 2), 1, 0)
    xb = 1 - core
    src_u = p == 0
    src_l = c < 2
    src_x = c == xb

    def at_y(off):
        return (lax.rem(y + off + NY, NY) * 2 + core, c)

    def at_z(off):
        return (r, lax.rem(z + off + NZ, NZ) * NX + x)

    def at_x(off):
        return (r, z * NX + lax.rem(x + off + NX, NX))

    barrier = pltpu.get_barrier_semaphore()

    def greet(device):
        pl.semaphore_signal(barrier, inc=1, device_id=device, device_id_type=MESH)

    for device in (at_y(1), at_y(-1), at_y(2), at_y(-2), at_x(1), at_x(-1), at_x(2), partner):
        greet(device)
    z_links = lambda k: [(k, child) for child in sorted(set(FAR.get(k, ())) | set(WIDE.get(k, ())))]
    down = [[child - k for _, child in z_links(k)] for k in range(NZ)]
    up = [[parent - k for parent in range(NZ) if (parent, k) in z_links(parent)] for k in range(NZ)]
    most_down, most_up = max(map(len, down)), max(map(len, up))
    z_down = [lut(z, [(d[i] + 4) % 8 - 4 if i < len(d) else 0 for d in down]) for i in range(most_down)]
    z_up = [lut(z, [(d[i] + 4) % 8 - 4 if i < len(d) else 0 for d in up]) for i in range(most_up)]
    n_down = lut(z, [len(d) for d in down])
    n_up = lut(z, [len(d) for d in up])
    for off in z_down:
        pl.when(hub & (off != 0))(lambda off=off: greet(at_z(off)))

    local = [
        pltpu.make_async_copy(linv, inv.at[0], loc.at[1]),
        pltpu.make_async_copy(uinv, inv.at[1], loc.at[2]),
        pltpu.make_async_copy(mat, M, loc.at[0]),
    ]
    own_rows = pltpu.make_async_copy(mat.at[pl.ds(0, NB)], U.at[core], loc.at[3])
    own_cols = pltpu.make_async_copy(mat.at[:, pl.ds(0, NB)], L.at[fb], loc.at[4])
    local[0].start()
    local[1].start()
    pl.when(src_u)(own_rows.start)
    pl.when(src_l)(own_cols.start)
    local[2].start()
    local[0].wait()
    local[1].wait()
    for k in range(4):
        high, low = split(inv[k // 2, k % 2])
        W[k, 0] = high
        W[k, 1] = low
    pl.when(src_u)(own_rows.wait)
    pl.when(src_l)(own_cols.wait)
    local[2].wait()
    pl.semaphore_wait(barrier, 8 + jnp.where(hub, n_up, 0))
    for off in z_up:

        @pl.when(hub & (off != 0))
        def _(off=off):
            pl.semaphore_signal(ready, inc=1, device_id=at_z(off), device_id_type=MESH)

    def u_part(ref, j):
        col = pl.multiple_of(j // 2 * 128, 128)
        row = pl.multiple_of(lax.rem(j, 2) * 128, 128)
        return ref.at[pl.ds(row, 128), pl.ds(col, 128)]

    def u_children(tree):
        out = []
        for slot in range(3):
            offs = offsets(tree, slot)
            if any(offs):
                off = lut(p, offs)
                out.append((slot, off != 0, at_y(sign * off)))
        return out

    def half(side):
        return pl.ds(pl.multiple_of(side * NB, NB), NB)

    def panel(q):
        cols = pl.ds(pl.multiple_of(q * NB, NB), NB)
        raw = U[core, :, cols]
        value = dot(W[core, 0], raw) + dot(W[core, 1], raw)
        UF[half(core), cols] = jnp.where((q > 0) | (c > 1), value, 0.0).astype(BF16)
        mine = UF.at[half(core), cols]
        remote(mine, mine, ps.at[0], pr.at[0], partner).start()

        @pl.when((r == 0) & ((q > 0) | (c > 0)))
        def _():
            M[0:NB, cols] = value.astype(BF16)

    sequences = []
    for g, (tree, first, count, start, rate, arrival) in enumerate(GROUPS):

        def own(j, g=g, first=first, tree=tree):
            j = j + first
            buf = u_part(U.at[core], j)

            @pl.when(jnp.logical_not(src_u))
            def _():
                remote(buf, buf, ur.at[j], ur.at[j], partner).wait_recv()

            for slot, cond, device in u_children(tree):
                pl.when(cond)(remote(buf, buf, us.at[g, slot], ur.at[j], device).start)

            @pl.when(lax.rem(j, 4) == 3)
            def _():
                panel(j // 4)

        sequences.append((start + lut(p, arrival), rate, count, own))

    def rows_of(j):
        return pl.ds(pl.multiple_of(j * LROWS, LROWS), LROWS)

    plane = []
    for slot in range(2):
        off = lut(z, offsets(FAR, slot))
        plane.append((hub & (off != 0), at_z(off)))
    plane.append((hub, at_x(1)))
    plane.append((hub | (x == 3), at_x(-1)))
    plane.append((x == 2, at_x(1)))
    plane_x = []
    for slot in range(3):
        off = lut(z, offsets(WIDE, slot))
        plane_x.append((off != 0, at_z(off)))
    plane_x += [(None, at_x(2)), (None, at_x(1)), (None, at_x(-1))]

    def when(cond, fn):
        if cond is None:
            fn()
        else:
            pl.when(cond)(fn)

    def from_hub(block):
        return jnp.where(block == 0, x, lax.rem(1 - x + NX, NX))

    def column(j):
        buf = L.at[fb, rows_of(j)]

        @pl.when(hub & (n_down > 0) & (j == 0))
        def _():
            pl.semaphore_wait(ready, n_down)

        @pl.when(jnp.logical_not(src_l))
        def _():
            remote(buf, buf, lr.at[fb, j], lr.at[fb, j], partner).wait_recv()

        for slot, (cond, device) in enumerate(plane):
            pl.when(cond)(remote(buf, buf, ls.at[slot], lr.at[fb, j], device).start)

    def corner(j):
        buf = X.at[core, rows_of(j)]

        @pl.when(src_x)
        def _():
            X[core, rows_of(j)] = U[core, rows_of(j), 0:NB]

        @pl.when(jnp.logical_not(src_x))
        def _():
            remote(buf, buf, xr.at[j], xr.at[j], partner).wait_recv()

        @pl.when(x == xb)
        def _():
            for slot, (cond, device) in enumerate(plane_x):
                when(cond, remote(buf, buf, xs.at[slot], xr.at[j], device).start)

        remote(buf, buf, xp.at[0], xq.at[0], partner).start()

    def lower(_):
        @pl.loop(0, LCH)
        def _(j):
            buf = L.at[1 - fb, rows_of(j)]
            remote(buf, buf, lr.at[1 - fb, j], lr.at[1 - fb, j], partner).wait_recv()

        for part in range(2):
            rows = pl.ds(part * NB, NB)
            raw0, raw1 = L[0, rows], L[1, rows]
            lower0 = dot(raw0, W[2, 0]) + dot(raw0, W[2, 1])
            LF[rows, 0:NB] = jnp.where(part * 16 + r > 0, lower0, 0.0).astype(BF16)
            D1[rows] = dot(raw1, W[3, 0]) + dot(raw1, W[3, 1])

    def corners(_):
        buf = X.at[1 - core]
        remote(buf, buf, xq.at[0], xq.at[0], partner).wait_recv()
        l10 = (dot(X[1], W[2, 0]) + dot(X[1], W[2, 1])).astype(BF16)
        u01 = (dot(W[0, 0], X[0]) + dot(W[0, 1], X[0])).astype(BF16)
        small[0] = (dot(W[1, 0], l10) + dot(W[1, 1], l10)).astype(BF16)
        small[1] = (dot(u01, W[3, 0]) + dot(u01, W[3, 1])).astype(BF16)
        small[2] = u01
        for part in range(2):
            rows = pl.ds(part * NB, NB)
            block = part * 16 + r
            lower0 = LF[rows, 0:NB]
            lower1 = D1[rows] - dot(lower0, small[1])
            lower1 = jnp.where(block > 1, lower1, 0.0).astype(BF16)

            @pl.when((c == 0) & (block > 0))
            def _():
                M[rows, 0:NB] = lower0

            @pl.when((c == 1) & (block > 1))
            def _():
                M[rows, 0:NB] = lower1

            if part == 0:

                @pl.when((c == 1) & (r == 1))
                def _():
                    M[rows, 0:NB] = (M[rows, 0:NB].astype(F32) - dot(lower0, small[2])).astype(BF16)

            LF[rows, 0:NB] = (lower0.astype(F32) - dot(lower1, small[0])).astype(BF16)
            LF[rows, NB : 2 * NB] = lower1

    from_z = lut(z, PLANE)
    from_x = jnp.maximum(lut(from_hub(0), (0, 5, 10, 6)), lut(from_hub(1), (0, 5, 10, 6)))
    sequences.append((from_z + lut(from_hub(fb), (0, 5, 10, 6)), 1, LCH, column))
    x_ready = jnp.maximum(LCH, 5 + lut(p, GROUPS[0][5])) + lut(z, PLANE_X)
    sequences.append((x_ready + lut(from_hub(xb), (0, 6, 7, 6)), 1, XCH, corner))
    sequences.append((from_z + from_x + LCH + 4, 1, 1, lower))
    sequences.append((jnp.maximum(from_z + from_x + LCH + 4, x_ready + 7 + XCH + 4), 1, 1, corners))

    def step(it, done):
        now = []
        for (start, rate, count, handle), begin in zip(sequences, done):
            end = jnp.clip((it + 1 - start) * rate, 0, count)
            end = jnp.where(it == STEPS - 1, count, end)
            lax.fori_loop(begin, end, lambda j, _, handle=handle: (handle(j), jnp.int32(0))[1], jnp.int32(0))
            now.append(end)
        return tuple(now)

    lax.fori_loop(0, STEPS, step, tuple(jnp.int32(0) for _ in sequences))

    theirs = UF.at[half(1 - core)]
    remote(theirs, theirs, pr.at[0], pr.at[0], partner).wait_recv()

    @pl.when(r == 1)
    def _():
        LF[0:NB] = jnp.zeros((NB, 2 * NB), BF16)

        @pl.loop(0, COLS // NB)
        def _(q):
            cols = pl.ds(pl.multiple_of(q * NB, NB), NB)
            raw = U[1, :, cols]

            @pl.when((q > 0) | (c > 1))
            def _():
                value = dot(W[1, 0], raw) + dot(W[1, 1], raw) - dot(small[0], UF[0:NB, cols])
                M[0:NB, cols] = value.astype(BF16)

    for g, (tree, first, count, _, _, _) in enumerate(GROUPS):
        buf = U.at[core, :, pl.ds(first * 64, count * 64)]
        for slot, cond, device in u_children(tree):
            pl.when(cond)(remote(buf, buf, us.at[g, slot], ur.at[0], device).wait_send)
    remote(theirs, theirs, ps.at[0], pr.at[0], partner).wait_send()
    for slot, (cond, device) in enumerate(plane):
        pl.when(cond)(remote(L.at[fb], L.at[fb], ls.at[slot], lr.at[fb, 0], device).wait_send)

    @pl.when(x == xb)
    def _():
        for slot, (cond, device) in enumerate(plane_x):
            when(cond, remote(X.at[core], X.at[core], xs.at[slot], xr.at[0], device).wait_send)

    remote(X.at[core], X.at[core], xp.at[0], xq.at[0], partner).wait_send()


def update(UF, LF, M, out, O, sems):
    copies = []
    for q in range(COLS // NB):
        cols = pl.ds(q * NB, NB)
        O[:, cols] = (M[:, cols].astype(F32) - dot(LF[...], UF[:, cols])).astype(BF16)
        copies.append(pltpu.make_async_copy(O.at[:, cols], out.at[:, cols], sems.at[q]))
        copies[-1].start()
    for copy in copies:
        copy.wait()


def body(matrix, lower_inv, upper_inv):
    D = pltpu.SemaphoreType.DMA
    vmem = pl.BlockSpec(memory_space=pltpu.VMEM)
    hbm = pl.BlockSpec(memory_space=pltpu.HBM)
    UF, LF, M = pl.pallas_call(
        gather,
        out_shape=(
            jax.ShapeDtypeStruct((2 * NB, COLS), BF16),
            jax.ShapeDtypeStruct((512, 2 * NB), BF16),
            jax.ShapeDtypeStruct((512, COLS), BF16),
        ),
        in_specs=[hbm] * 3,
        out_specs=(vmem, vmem, vmem),
        scratch_shapes=[
            pltpu.VMEM((2, NB, COLS), BF16),
            pltpu.VMEM((2, NB, NB), BF16),
            pltpu.VMEM((2, 512, NB), BF16),
            pltpu.VMEM((2, 2, NB, NB), F32),
            pltpu.VMEM((4, 2, NB, NB), BF16),
            pltpu.VMEM((3, NB, NB), BF16),
            pltpu.VMEM((512, NB), F32),
            D((3, 3)),
            D((UCH,)),
            D((1,)),
            D((1,)),
            D((5,)),
            D((2, LCH)),
            D((6,)),
            D((XCH,)),
            D((1,)),
            D((1,)),
            pltpu.SemaphoreType.REGULAR,
            D((5,)),
        ],
        compiler_params=pltpu.CompilerParams(
            collective_id=0, has_side_effects=True, vmem_limit_bytes=32 * 2**20
        ),
    )(*(pltpu.with_memory_space_constraint(a, pltpu.HBM) for a in (matrix, lower_inv, upper_inv)))
    return pl.pallas_call(
        update,
        out_shape=jax.ShapeDtypeStruct(matrix.shape, matrix.dtype),
        in_specs=[vmem] * 3,
        out_specs=hbm,
        scratch_shapes=[pltpu.VMEM((512, COLS), BF16), D((COLS // NB,))],
        compiler_params=pltpu.CompilerParams(vmem_limit_bytes=16 * 2**20),
    )(UF, LF, M)


def solution(mesh):
    in_specs = (P("row", "col"), P(), P())
    return jax.shard_map(body, mesh=mesh, in_specs=in_specs, out_specs=P("row", "col"), check_vma=False)
```

```python
import jax
import jax.numpy as jnp
from jax import lax
from jax.experimental import pallas as pl
from jax.experimental.pallas import tpu as pltpu
from jax.sharding import PartitionSpec as P

MESH = pl.DeviceIdType.MESH
F32 = jnp.float32
BF16 = jnp.bfloat16
NB = 256
COLS = 1792
NY, NZ, NX = 8, 8, 4

NEAR = {0: (1, 7), 1: (2,), 2: (3,), 3: (4,), 7: (6,), 6: (5,)}
FAR = {0: (2, 6), 2: (1, 3), 3: (4,), 6: (7, 5)}
WIDE = {0: (2, 6), 2: (4, 3, 1), 6: (5, 7)}
LONG = {0: (2,), 2: (3, 1), 3: (4,), 4: (5,), 5: (6,), 6: (7,)}

GROUPS = (
    (FAR, 0, 4, 0, 1, (0, 8, 5, 8, 11, 8, 5, 8)),
    (LONG, 4, 16, 4, 2, (-4, 8, 4, 8, 11, 15, 18, 21)),
    (NEAR, 20, 8, 12, 1, (-8, 4, 7, 10, 14, 10, 7, 4)),
)
UCH = 28
SHARED = 5
LROWS = 64
LCH = 1024 // LROWS
XCH = NB // LROWS
STEPS = 36
LOWER_AT = 30
PLANE = (0, 10, 6, 10, 15, 10, 6, 10)
FROM_HUB = (0, 5, 10, 6)
PLANE_X = (0, 10, 6, 10, 11, 9, 6, 9)


def offsets(tree, slot):
    out = []
    for k in range(8):
        children = tree.get(k, ())
        out.append((children[slot] - k + 4) % 8 - 4 if slot < len(children) else 0)
    return out


def lut(index, values):
    result = jnp.int32(values[0])
    for k in range(1, len(values)):
        if values[k] != values[0]:
            result = jnp.where(index == k, jnp.int32(values[k]), result)
    return result


def split(value):
    high = value.astype(BF16)
    return high, (value - high.astype(F32)).astype(BF16)


def dot(a, b):
    return jnp.dot(a, b, preferred_element_type=F32)


def remote(src, dst, send, recv, device):
    return pltpu.make_async_remote_copy(
        src_ref=src, dst_ref=dst, send_sem=send, recv_sem=recv, device_id=device, device_id_type=MESH
    )


def gather(
    mat, linv, uinv, UF, LF, M, U, X, L, inv, W, small, D1, us, ur, ps, pr, fs, fr, ls, lr, ll, lq, xs, xr, xl, xq, B1, ready, loc
):
    r = lax.axis_index("row")
    c = lax.axis_index("col")
    y, core = r // 2, lax.rem(r, 2)
    z, x = c // NX, lax.rem(c, NX)
    partner = (y * 2 + 1 - core, c)
    first_core = core == 0
    hub = x < 2
    fb = jnp.where((x == 1) | (x == 2), 1, 0)
    hb = jnp.where(x == 0, 1, 0)
    turn = jnp.where(lax.rem(x, 2) == 0, 1, -1)
    src_l = c < 2

    def at_y(off, to_core):
        return (lax.rem(y + off + NY, NY) * 2 + to_core, c)

    def at_z(off):
        return (r, lax.rem(z + off + NZ, NZ) * NX + x)

    def at_x(off, to_core):
        return (y * 2 + to_core, z * NX + lax.rem(x + off + NX, NX))

    def u_part(ref, j):
        col = pl.multiple_of(j // 2 * 128, 128)
        row = pl.multiple_of(lax.rem(j, 2) * 128, 128)
        return ref.at[pl.ds(row, 128), pl.ds(col, 128)]

    def block(q):
        return pl.ds(pl.multiple_of(q * NB, NB), NB)

    barrier = pltpu.get_barrier_semaphore()

    def greet(device):
        pl.semaphore_signal(barrier, inc=1, device_id=device, device_id_type=MESH)

    z_links = [(k, child) for k in range(NZ) for child in sorted(set(FAR.get(k, ())) | set(WIDE.get(k, ())))]
    down = [[child - k for k, child in z_links if k == at] for at in range(NZ)]
    up = [[k - child for k, child in z_links if child == at] for at in range(NZ)]
    z_down = [lut(z, [(d[i] + 4) % 8 - 4 if i < len(d) else 0 for d in down]) for i in range(max(map(len, down)))]
    z_up = [lut(z, [(d[i] + 4) % 8 - 4 if i < len(d) else 0 for d in up]) for i in range(max(map(len, up)))]
    n_down = lut(z, [len(d) for d in down])
    n_up = lut(z, [len(d) for d in up])
    rank = [[down[(at + off) % NZ].index(-off) for off in d] for at, d in enumerate(up)]
    z_rank = [lut(z, [k[i] if i < len(k) else 0 for k in rank]) for i in range(len(z_up))]

    greet(partner)
    greet(at_x(turn, 0))

    @pl.when(first_core)
    def _():
        pl.when(x != 0)(lambda: greet(at_x(-x, 0)))
        pl.when(x != 1)(lambda: greet(at_x(1 - x, 0)))
        pl.when(x >= 2)(lambda: greet(at_x(-turn, 0)))
        for off in z_down:
            pl.when(hub & (off != 0))(lambda off=off: greet(at_z(off)))

    @pl.when(core == 1)
    def _():
        for off in (1, -1, 2, -2):
            greet(at_y(off, 1))
        pl.when((y == 1) | (y == 2) | (y == 6) | (y == 7))(lambda: greet((0, c)))

    local = [
        pltpu.make_async_copy(linv, inv.at[0], loc.at[1]),
        pltpu.make_async_copy(uinv, inv.at[1], loc.at[2]),
        pltpu.make_async_copy(mat, M, loc.at[0]),
    ]
    mine = pl.ds(pl.multiple_of(core * 512, 512), 512)
    own_rows = pltpu.make_async_copy(mat.at[pl.ds(0, NB)], U.at[core], loc.at[3])
    own_cols = pltpu.make_async_copy(mat.at[:, pl.ds(0, NB)], L.at[mine], loc.at[4])
    local[0].start()
    local[1].start()
    pl.when(y == 0)(own_rows.start)
    pl.when(src_l)(own_cols.start)
    local[2].start()
    count_0 = 3 + jnp.where(hub, 4 + n_up, 0) + jnp.where(y == 0, 4, 0)
    pl.semaphore_wait(barrier, jnp.where(first_core, count_0, 5))

    @pl.when(y == 0)
    def _():
        for side in range(2):

            @pl.when(core == side)
            def _(side=side):
                for g, (tree, first, count, _, _, _) in enumerate(GROUPS):

                    @pl.loop(first, first + count)
                    def _(j, g=g, tree=tree):
                        for slot, child in enumerate(tree[0]):
                            off = child if child <= 4 else child - 8
                            remote(
                                u_part(mat, j),
                                u_part(U.at[side], j),
                                us.at[side, g, slot],
                                ur.at[side, j],
                                at_y(off if side == 0 else -off, 1),
                            ).start()

                if side == 1:

                    @pl.loop(0, 7)
                    def _(q):
                        raw = mat.at[pl.ds(0, NB), block(q)]
                        remote(raw, U.at[1, :, block(q)], ps.at[1], pr.at[1, q], partner).start()

                else:
                    remote(mat.at[pl.ds(0, NB)], U.at[0], ps.at[0], pr.at[0, 0], partner).start()

    for off, place in zip(z_up, z_rank):

        @pl.when(first_core & hub & (off != 0))
        def _(off=off, place=place):
            pl.semaphore_signal(ready.at[place], inc=1, device_id=at_z(off), device_id_type=MESH)

    local[0].wait()
    local[1].wait()
    for k in range(4):
        high, low = split(inv[k // 2, k % 2])
        W[k, 0] = high
        W[k, 1] = low
    pl.when(y == 0)(own_rows.wait)
    pl.when(src_l)(own_cols.wait)
    local[2].wait()

    positions = (y, lax.rem(NY - y, NY))

    def u_children(side, tree):
        out = []
        for slot in range(2):
            offs = offsets(tree, slot)
            if any(offs):
                off = lut(positions[side], offs)
                out.append((slot, off != 0, at_y(off if side == 0 else -off, 1)))
        return out

    def panel(side, q):
        cols = block(q)
        raw = U[side, :, cols]
        value = dot(W[side, 0], raw) + dot(W[side, 1], raw)
        UF[block(side), cols] = jnp.where((q > 0) | (c > 1), value, 0.0).astype(BF16)

        @pl.when((r == 0) & (side == 0) & ((q > 0) | (c > 0)))
        def _():
            M[0:NB, cols] = value.astype(BF16)

    def hand_on(side, g, first, tree):
        def event(j):
            j = j + first
            buf = u_part(U.at[side], j)
            remote(buf, buf, ur.at[side, j], ur.at[side, j], partner).wait_recv()
            for slot, cond, device in u_children(side, tree):
                pl.when(cond)(remote(buf, buf, us.at[side, g, slot], ur.at[side, j], device).start)

            @pl.when(lax.rem(j, 4) == 3)
            def _():
                q = j // 4
                raw = U.at[side, :, block(q)]
                remote(raw, raw, ps.at[side], pr.at[side, q], partner).start()
                if first >= 4 * SHARED:
                    panel(side, q)

        return event

    def take(side, q):
        @pl.when((y != 0) | (side == 1))
        def _():
            raw = U.at[side, :, block(q)]
            remote(raw, raw, pr.at[side, q], pr.at[side, q], partner).wait_recv()

        panel(side, q)

    def take_and_give(side, q):
        take(side, q)
        done = UF.at[block(side), block(q)]
        remote(done, done, fs.at[0], fr.at[0], partner).start()

    on_1 = []
    for side in range(2):
        for g, (tree, first, count, start, rate, arrival) in enumerate(GROUPS):
            on_1.append((start + lut(positions[side], arrival), rate, count // rate, hand_on(side, g, first, tree)))

    def rows_of(j, base=0):
        return pl.ds(pl.multiple_of(base + j * LROWS, LROWS), LROWS)

    plane = []
    for slot in range(2):
        off = lut(z, offsets(FAR, slot))
        plane.append((hub & (off != 0), at_z(off)))
    plane.append((hub, at_x(-turn, 0)))
    plane_x = []
    for slot in range(3):
        off = lut(z, offsets(WIDE, slot))
        plane_x.append((off != 0, at_z(off)))

    def from_hub(side):
        return jnp.where(side == 0, x, lax.rem(1 - x + NX, NX))

    def column(j, slots):
        buf = L.at[rows_of(j)]

        @pl.when(jnp.logical_not(src_l))
        def _():
            remote(buf, buf, lr.at[j], lr.at[j], partner).wait_recv()

        for slot, (cond, device) in enumerate(plane):
            if slot in slots:
                pl.when(cond)(remote(buf, buf, ls.at[slot], lr.at[j], device).start)
        if 3 in slots:
            kept = L.at[rows_of(lax.rem(j, LCH // 2), 1024)]
            remote(buf, kept, ls.at[3], ll.at[0], at_x(turn, j // (LCH // 2))).start()

            @pl.when(jnp.logical_not(src_l) & (j >= LCH // 2))
            def _():
                remote(buf, buf, ls.at[4], lq.at[0], partner).start()

    def answered(place):
        @pl.when(hub & (n_down > place))
        def _():
            pl.semaphore_wait(ready.at[place], 1)

    def columns():
        @pl.when(src_l)
        def _():
            pl.loop(0, LCH // 2)(lambda j: column(j, (2, 3)))
            theirs = L.at[pl.ds(512, 512)]
            remote(theirs, theirs, lq.at[0], lq.at[0], partner).wait_recv()
            pl.loop(LCH // 2, LCH)(lambda j: column(j, (2, 3)))
            for slot in range(2):
                answered(slot)
                pl.loop(0, LCH)(lambda j: column(j, (slot,)))

        @pl.when(jnp.logical_not(src_l))
        def _():
            for place in range(3):
                answered(place)
            pl.loop(0, LCH)(lambda j: column(j, (0, 1, 2, 3)))

    def corner(j):
        buf = X.at[hb, rows_of(j)]

        @pl.when(z == 0)
        def _():
            X[hb, rows_of(j)] = U[hb, rows_of(j), 0:NB]

        @pl.when(z != 0)
        def _():
            remote(buf, buf, xr.at[j], xr.at[j], partner).wait_recv()

        for slot, (cond, device) in enumerate(plane_x):
            pl.when(cond)(remote(buf, buf, xs.at[slot], xr.at[j], device).start)
        for slot, off in enumerate((2, 1, -1)):
            remote(buf, buf, xs.at[3 + slot], xl.at[hb], at_x(off, 0)).start()

    def lower_rows(which, base):
        @pl.when(which == 0)
        def _():
            for part in range(2):
                raw = L[pl.ds(pl.multiple_of(base + part * NB, NB), NB)]
                value = dot(raw, W[2, 0]) + dot(raw, W[2, 1])
                LF[part * NB : (part + 1) * NB, 0:NB] = jnp.where(part * 16 + r > 0, value, 0.0).astype(BF16)

        @pl.when(which == 1)
        def _():
            for part in range(2):
                raw = L[pl.ds(pl.multiple_of(base + part * NB, NB), NB)]
                D1[part * NB : (part + 1) * NB] = dot(raw, W[3, 0]) + dot(raw, W[3, 1])

    def lower():
        @pl.when((core == 1) & jnp.logical_not(src_l))
        def _():
            remote(L.at[mine], L.at[mine], lq.at[0], lq.at[0], partner).wait_recv()

        lower_rows(fb, core * 512)
        kept = L.at[pl.ds(1024, 512)]
        remote(kept, kept, ll.at[0], ll.at[0], partner).wait_recv()
        lower_rows(1 - fb, 1024)

    def corners():
        @pl.when(first_core)
        def _():
            for k in range(2):

                @pl.when(x != 1 - k)
                def _():
                    remote(X.at[k], X.at[k], xl.at[k], xl.at[k], partner).wait_recv()

            remote(X, X, xs.at[6], xq.at[0], partner).start()

        @pl.when(core == 1)
        def _():
            remote(X, X, xq.at[0], xq.at[0], partner).wait_recv()

        l10 = (dot(X[1], W[2, 0]) + dot(X[1], W[2, 1])).astype(BF16)
        u01 = (dot(W[0, 0], X[0]) + dot(W[0, 1], X[0])).astype(BF16)
        small[0] = (dot(W[1, 0], l10) + dot(W[1, 1], l10)).astype(BF16)
        small[1] = (dot(u01, W[3, 0]) + dot(u01, W[3, 1])).astype(BF16)
        small[2] = u01
        for part in range(2):
            rows = pl.ds(part * NB, NB)
            at = part * 16 + r
            lower0 = LF[rows, 0:NB]
            lower1 = D1[rows] - dot(lower0, small[1])
            lower1 = jnp.where(at > 1, lower1, 0.0).astype(BF16)

            @pl.when((c == 0) & (at > 0))
            def _():
                M[rows, 0:NB] = lower0

            @pl.when((c == 1) & (at > 1))
            def _():
                M[rows, 0:NB] = lower1

            if part == 0:

                @pl.when((c == 1) & (r == 1))
                def _():
                    M[rows, 0:NB] = (M[rows, 0:NB].astype(F32) - dot(lower0, small[2])).astype(BF16)

            LF[rows, 0:NB] = (lower0.astype(F32) - dot(lower1, small[0])).astype(BF16)
            LF[rows, NB : 2 * NB] = lower1

    def steps(begin, end):
        @pl.loop(begin, end)
        def _(it):
            for start, rate, count, handle in on_1:
                k = it - start

                @pl.when((k >= 0) & (k < count))
                def _(k=k, rate=rate, handle=handle):
                    for i in range(rate):
                        handle(k * rate + i)

    @pl.when(first_core)
    def _():
        early = (y == 0) & (z != 0)
        near_side = jnp.where(y <= 4, 0, 1)

        def first_blocks():
            take_and_give(0, 0)
            take_and_give(1, 0)

        def near_blocks():
            pl.loop(1, SHARED)(lambda q: take_and_give(near_side, q))

        def far_blocks():
            @pl.loop(SHARED, 7)
            def _(q):
                take(0, q)
                take(1, q)

            pl.loop(1, SHARED)(lambda q: take_and_give(1 - near_side, q))

        @pl.when(early)
        def _():
            first_blocks()
            near_blocks()
            far_blocks()

        columns()
        pl.when(jnp.logical_not(early))(first_blocks)

        @pl.when(hub)
        def _():
            pl.loop(0, XCH)(corner)

        lower()
        pl.when(jnp.logical_not(early))(near_blocks)
        corners()
        pl.when(jnp.logical_not(early))(far_blocks)

        for g, (tree, first, count, _, _, _) in enumerate(GROUPS):
            buf = U.at[0, :, pl.ds(first * 64, count * 64)]
            for slot, cond, device in u_children(0, tree):
                pl.when(cond & (y == 0))(remote(buf, buf, us.at[0, g, slot], ur.at[0, 0], device).wait_send)
        pl.when(y == 0)(remote(U.at[0], U.at[0], ps.at[0], pr.at[0, 0], partner).wait_send)
        shared = UF.at[:, pl.ds(0, SHARED * NB)]
        remote(shared, shared, fs.at[0], fr.at[0], partner).wait_send()
        whole = L.at[pl.ds(0, 1024)]
        for slot, (cond, device) in enumerate(plane):
            pl.when(cond)(remote(whole, whole, ls.at[slot], lr.at[0], device).wait_send)
        remote(whole, whole, ls.at[3], ll.at[0], partner).wait_send()
        part = L.at[pl.ds(512, 512)]
        pl.when(jnp.logical_not(src_l))(remote(part, part, ls.at[4], lq.at[0], partner).wait_send)

        @pl.when(hub)
        def _():
            for slot, (cond, device) in enumerate(plane_x):
                pl.when(cond)(remote(X.at[0], X.at[0], xs.at[slot], xr.at[0], device).wait_send)
            for slot in range(3):
                remote(X.at[0], X.at[0], xs.at[3 + slot], xl.at[0], partner).wait_send()

        remote(X, X, xs.at[6], xq.at[0], partner).wait_send()

    @pl.when(core == 1)
    def _():
        mine_1 = L.at[pl.ds(512, 512)]
        give = remote(mine_1, mine_1, ls.at[4], lq.at[0], partner)
        pl.when(src_l)(give.start)
        @pl.when(y == 0)
        def _():
            @pl.loop(0, 7)
            def _(q):
                raw = U[1, :, block(q)]
                value = dot(W[1, 0], raw) + dot(W[1, 1], raw)
                B1[:, block(q)] = value

                @pl.when(q >= SHARED)
                def _():
                    UF[NB : 2 * NB, block(q)] = value.astype(BF16)

            remote(U.at[0], U.at[0], pr.at[0, 0], pr.at[0, 0], partner).wait_recv()
            pl.loop(SHARED, 7)(lambda q: panel(0, q))

        pl.when(y != 0)(lambda: steps(0, LOWER_AT))
        lower()
        pl.when(y != 0)(lambda: steps(LOWER_AT, STEPS))
        corners()
        shared = UF.at[:, pl.ds(0, SHARED * NB)]
        remote(shared, shared, fr.at[0], fr.at[0], partner).wait_recv()

        @pl.when(y == 0)
        def _():
            LF[0:NB] = jnp.zeros((NB, 2 * NB), BF16)

            @pl.loop(0, COLS // NB)
            def _(q):
                cols = block(q)

                @pl.when((q > 0) | (c > 1))
                def _():
                    M[0:NB, cols] = (B1[:, cols] - dot(small[0], UF[0:NB, cols])).astype(BF16)

        for side in range(2):
            for g, (tree, first, count, _, _, _) in enumerate(GROUPS):
                buf = U.at[side, :, pl.ds(first * 64, count * 64)]
                for slot, cond, device in u_children(side, tree):
                    sent = cond if side == 1 else cond & (y != 0)
                    pl.when(sent)(remote(buf, buf, us.at[side, g, slot], ur.at[side, 0], device).wait_send)
            sent = remote(U.at[side], U.at[side], ps.at[side], pr.at[side, 0], partner)
            if side == 1:
                sent.wait_send()
            else:
                pl.when(y != 0)(sent.wait_send)
        pl.when(src_l)(give.wait_send)


def update(UF, LF, M, out, O, sems):
    copies = []
    for q in range(COLS // NB):
        cols = pl.ds(q * NB, NB)
        O[:, cols] = (M[:, cols].astype(F32) - dot(LF[...], UF[:, cols])).astype(BF16)
        copies.append(pltpu.make_async_copy(O.at[:, cols], out.at[:, cols], sems.at[q]))
        copies[-1].start()
    for copy in copies:
        copy.wait()


def body(matrix, lower_inv, upper_inv):
    D = pltpu.SemaphoreType.DMA
    vmem = pl.BlockSpec(memory_space=pltpu.VMEM)
    hbm = pl.BlockSpec(memory_space=pltpu.HBM)
    UF, LF, M = pl.pallas_call(
        gather,
        out_shape=(
            jax.ShapeDtypeStruct((2 * NB, COLS), BF16),
            jax.ShapeDtypeStruct((512, 2 * NB), BF16),
            jax.ShapeDtypeStruct((512, COLS), BF16),
        ),
        in_specs=[hbm] * 3,
        out_specs=(vmem, vmem, vmem),
        scratch_shapes=[
            pltpu.VMEM((2, NB, COLS), BF16),
            pltpu.VMEM((2, NB, NB), BF16),
            pltpu.VMEM((1536, NB), BF16),
            pltpu.VMEM((2, 2, NB, NB), F32),
            pltpu.VMEM((4, 2, NB, NB), BF16),
            pltpu.VMEM((3, NB, NB), BF16),
            pltpu.VMEM((512, NB), F32),
            D((2, 3, 2)),
            D((2, UCH)),
            D((2,)),
            D((2, 7)),
            D((1,)),
            D((1,)),
            D((5,)),
            D((LCH,)),
            D((1,)),
            D((1,)),
            D((7,)),
            D((XCH,)),
            D((2,)),
            D((1,)),
            pltpu.VMEM((NB, COLS), F32),
            pltpu.SemaphoreType.REGULAR((3,)),
            D((5,)),
        ],
        compiler_params=pltpu.CompilerParams(
            collective_id=0, has_side_effects=True, vmem_limit_bytes=32 * 2**20
        ),
    )(*(pltpu.with_memory_space_constraint(a, pltpu.HBM) for a in (matrix, lower_inv, upper_inv)))
    return pl.pallas_call(
        update,
        out_shape=jax.ShapeDtypeStruct(matrix.shape, matrix.dtype),
        in_specs=[vmem] * 3,
        out_specs=hbm,
        scratch_shapes=[pltpu.VMEM((512, COLS), BF16), D((COLS // NB,))],
        compiler_params=pltpu.CompilerParams(vmem_limit_bytes=16 * 2**20),
    )(UF, LF, M)


def solution(mesh):
    in_specs = (P("row", "col"), P(), P())
    return jax.shard_map(body, mesh=mesh, in_specs=in_specs, out_specs=P("row", "col"), check_vma=False)
```

```python
import jax
import jax.numpy as jnp
from jax import lax
from jax.experimental import pallas as pl
from jax.experimental.pallas import tpu as pltpu
from jax.sharding import PartitionSpec as P

MESH = pl.DeviceIdType.MESH
F32 = jnp.float32
BF16 = jnp.bfloat16
NB = 256
COLS = 1792
NY, NZ, NX = 8, 8, 4

NEAR = {0: (1, 7), 1: (2,), 2: (3,), 3: (4,), 7: (6,), 6: (5,)}
FAR = {0: (2, 6), 2: (1, 3), 3: (4,), 6: (7, 5)}
WIDE = {0: (2, 6), 2: (4, 3, 1), 6: (5, 7)}
LONG = {0: (2,), 2: (3, 1), 3: (4,), 4: (5,), 5: (6,), 6: (7,)}

GROUPS = (
    (LONG, 0, 4, 0, 2, (0, 8, 5, 8, 11, 15, 18, 21)),
    (LONG, 4, 16, 2, 2, (0, 8, 5, 8, 11, 15, 18, 21)),
    (NEAR, 20, 8, 10, 1, (0, 4, 7, 10, 14, 10, 7, 4)),
)
FIRST = (FAR, (0, 8, 5, 8, 11, 8, 5, 8))
UCH = 28
SHARED = 5
LROWS = 64
LCH = 1024 // LROWS
XCH = NB // LROWS
STEPS = 36
LOWER_AT = (28, 24, 28, 28, 23, 28, 28, 24)
CORNERS_AT = (31, 28, 31, 31, 28, 31, 31, 28)
PLANE = (0, 10, 6, 10, 15, 10, 6, 10)
FROM_HUB = (0, 5, 10, 6)
PLANE_X = (0, 10, 6, 10, 11, 9, 6, 9)


def offsets(tree, slot):
    out = []
    for k in range(8):
        children = tree.get(k, ())
        out.append((children[slot] - k + 4) % 8 - 4 if slot < len(children) else 0)
    return out


def lut(index, values):
    result = jnp.int32(values[0])
    for k in range(1, len(values)):
        if values[k] != values[0]:
            result = jnp.where(index == k, jnp.int32(values[k]), result)
    return result


def split(value):
    high = value.astype(BF16)
    return high, (value - high.astype(F32)).astype(BF16)


def dot(a, b):
    return jnp.dot(a, b, preferred_element_type=F32)


def remote(src, dst, send, recv, device):
    return pltpu.make_async_remote_copy(
        src_ref=src, dst_ref=dst, send_sem=send, recv_sem=recv, device_id=device, device_id_type=MESH
    )


def gather(
    mat, linv, uinv, UF, LF, M, U, X, L, inv, W, small, D1, us, ur, ps, pr, fs, fr, ls, lr, ll, lq, xs, xr, xl, xq, B1, ready, answer, loc
):
    r = lax.axis_index("row")
    c = lax.axis_index("col")
    y, core = r // 2, lax.rem(r, 2)
    z, x = c // NX, lax.rem(c, NX)
    partner = (y * 2 + 1 - core, c)
    first_core = core == 0
    hub = x < 2
    fb = jnp.where((x == 1) | (x == 2), 1, 0)
    hb = jnp.where(x == 0, 1, 0)
    turn = jnp.where(lax.rem(x, 2) == 0, 1, -1)
    src_l = c < 2

    def at_y(off, to_core):
        return (lax.rem(y + off + NY, NY) * 2 + to_core, c)

    def at_z(off):
        return (r, lax.rem(z + off + NZ, NZ) * NX + x)

    def at_x(off, to_core):
        return (y * 2 + to_core, z * NX + lax.rem(x + off + NX, NX))

    def u_part(ref, j):
        col = pl.multiple_of(j // 2 * 128, 128)
        row = pl.multiple_of(lax.rem(j, 2) * 128, 128)
        return ref.at[pl.ds(row, 128), pl.ds(col, 128)]

    def block(q):
        return pl.ds(pl.multiple_of(q * NB, NB), NB)

    barrier = pltpu.get_barrier_semaphore()

    def greet(device):
        pl.semaphore_signal(barrier, inc=1, device_id=device, device_id_type=MESH)

    z_links = [(k, child) for k in range(NZ) for child in sorted(set(FAR.get(k, ())) | set(WIDE.get(k, ())))]
    down = [[child - k for k, child in z_links if k == at] for at in range(NZ)]
    up = [[k - child for k, child in z_links if child == at] for at in range(NZ)]
    z_down = [lut(z, [(d[i] + 4) % 8 - 4 if i < len(d) else 0 for d in down]) for i in range(max(map(len, down)))]
    z_up = [lut(z, [(d[i] + 4) % 8 - 4 if i < len(d) else 0 for d in up]) for i in range(max(map(len, up)))]
    n_down = lut(z, [len(d) for d in down])
    n_up = lut(z, [len(d) for d in up])
    rank = [[down[(at + off) % NZ].index(-off) for off in d] for at, d in enumerate(up)]
    z_rank = [lut(z, [k[i] if i < len(k) else 0 for k in rank]) for i in range(len(z_up))]

    @pl.when(core == 1)
    def _():
        for off in (1, -1, 2, -2):
            greet(at_y(off, 1))
        pl.when((y == 1) | (y == 2) | (y == 6) | (y == 7))(lambda: greet((0, c)))

    pl.when(core == 1)(lambda: greet(partner))
    greet(at_x(turn, 0))

    @pl.when(first_core)
    def _():
        pl.when(x != 0)(lambda: greet(at_x(-x, 0)))
        pl.when(x != 1)(lambda: greet(at_x(1 - x, 0)))
        pl.when(x >= 2)(lambda: greet(at_x(-turn, 0)))
        for off in z_down:
            pl.when(hub & (off != 0))(lambda off=off: greet(at_z(off)))

    local = [
        pltpu.make_async_copy(linv, inv.at[0], loc.at[1]),
        pltpu.make_async_copy(uinv, inv.at[1], loc.at[2]),
        pltpu.make_async_copy(mat, M, loc.at[0]),
    ]
    mine = pl.ds(pl.multiple_of(core * 512, 512), 512)
    own_rows = pltpu.make_async_copy(mat.at[pl.ds(0, NB)], U.at[core], loc.at[3])
    own_cols = pltpu.make_async_copy(mat.at[:, pl.ds(0, NB)], L.at[mine], loc.at[4])
    local[0].start()
    local[1].start()
    pl.when(y == 0)(own_rows.start)
    pl.when(src_l)(own_cols.start)
    local[2].start()
    count_0 = 3 + jnp.where(hub, 4 + n_up, 0) + jnp.where(y == 0, 4, 0)
    pl.semaphore_wait(barrier, jnp.where(first_core, count_0, 4))

    @pl.when(first_core)
    def _():
        pl.semaphore_signal(answer, inc=1, device_id=partner, device_id_type=MESH)


    near_side = jnp.where(y <= 4, 0, 1)
    positions = (y, lax.rem(NY - y, NY))
    def u_children(side, g):
        out = []
        for slot in range(2):
            offs = offsets(GROUPS[g][0], slot)
            fast = offsets(FIRST[0], slot) if g == 0 else offs
            if any(offs) or any(fast):
                off = lut(positions[side], offs)
                if g == 0:
                    off = jnp.where(c == 1 - side, lut(positions[side], fast), off)
                out.append((slot, off != 0, at_y(off if side == 0 else -off, 1)))
        return out

    children = [[u_children(side, g) for g in range(len(GROUPS))] for side in range(2)]


    @pl.when(y == 0)
    def _():
        for side in range(2):

            @pl.when(core == side)
            def _(side=side):
                for g, (tree, first, count, _, _, _) in enumerate(GROUPS):

                    @pl.loop(first, first + count)
                    def _(j, g=g):
                        for slot, cond, device in children[side][g]:
                            there = u_part(U.at[side], j)
                            copy = remote(u_part(mat, j), there, us.at[side, g, slot], ur.at[side, j], device)
                            pl.when(cond)(copy.start)

                if side == 1:
                    pl.semaphore_wait(answer, 1)

                    @pl.loop(0, 7)
                    def _(q):
                        raw = mat.at[pl.ds(0, NB), block(q)]
                        remote(raw, U.at[1, :, block(q)], ps.at[1], pr.at[1, q], partner).start()

                else:
                    remote(mat.at[pl.ds(0, NB)], U.at[0], ps.at[0], pr.at[0, 0], partner).start()

    for off, place in zip(z_up, z_rank):

        @pl.when(first_core & hub & (off != 0))
        def _(off=off, place=place):
            pl.semaphore_signal(ready.at[place], inc=1, device_id=at_z(off), device_id_type=MESH)

    local[0].wait()
    local[1].wait()
    for k in range(4):
        high, low = split(inv[k // 2, k % 2])
        W[k, 0] = high
        W[k, 1] = low
    pl.when(y == 0)(own_rows.wait)
    pl.when(src_l)(own_cols.wait)
    local[2].wait()

    @pl.when((core == 1) & (y != 0))
    def _():
        pl.semaphore_wait(answer, 1)

    def panel(side, q):
        cols = block(q)
        raw = U[side, :, cols]
        value = dot(W[side, 0], raw) + dot(W[side, 1], raw)
        UF[block(side), cols] = jnp.where((q > 0) | (c > 1), value, 0.0).astype(BF16)

        @pl.when((r == 0) & (side == 0) & ((q > 0) | (c > 0)))
        def _():
            M[0:NB, cols] = value.astype(BF16)

    def hand_on(side, g, first, tree):
        def event(j):
            j = j + first
            buf = u_part(U.at[side], j)
            remote(buf, buf, ur.at[side, j], ur.at[side, j], partner).wait_recv()
            for slot, cond, device in children[side][g]:
                pl.when(cond)(remote(buf, buf, us.at[side, g, slot], ur.at[side, j], device).start)

            @pl.when(lax.rem(j, 4) == 3)
            def _():
                q = j // 4
                raw = U.at[side, :, block(q)]
                remote(raw, raw, ps.at[side], pr.at[side, q], partner).start()
                if first >= 4 * SHARED:
                    panel(side, q)
                else:
                    pl.when(side != near_side)(lambda: panel(side, q))

        return event

    def take(side, q):
        @pl.when((y != 0) | (side == 1))
        def _():
            raw = U.at[side, :, block(q)]
            remote(raw, raw, pr.at[side, q], pr.at[side, q], partner).wait_recv()

        panel(side, q)

    def take_and_give(side, q):
        take(side, q)
        done = UF.at[block(side), block(q)]
        remote(done, done, fs.at[0], fr.at[0], partner).start()

    on_1 = []
    for side in range(2):
        for g, (tree, first, count, start, rate, arrival) in enumerate(GROUPS):
            at = lut(positions[side], arrival)
            if g == 0:
                at = jnp.where(c == 1 - side, lut(positions[side], FIRST[1]), at)
            on_1.append((start + at, rate, count // rate, hand_on(side, g, first, tree)))

    def rows_of(j, base=0):
        return pl.ds(pl.multiple_of(base + j * LROWS, LROWS), LROWS)

    plane = []
    for slot in range(2):
        off = lut(z, offsets(FAR, slot))
        plane.append((hub & (off != 0), at_z(off)))
    plane.append((hub, at_x(-turn, 0)))
    plane_x = []
    for slot in range(3):
        off = lut(z, offsets(WIDE, slot))
        plane_x.append((off != 0, at_z(off)))

    def from_hub(side):
        return jnp.where(side == 0, x, lax.rem(1 - x + NX, NX))

    def column(j, slots):
        buf = L.at[rows_of(j)]

        @pl.when(jnp.logical_not(src_l))
        def _():
            remote(buf, buf, lr.at[j], lr.at[j], partner).wait_recv()

        for slot, (cond, device) in enumerate(plane):
            if slot in slots:
                pl.when(cond)(remote(buf, buf, ls.at[slot], lr.at[j], device).start)
        if 3 in slots:
            kept = L.at[rows_of(lax.rem(j, LCH // 2), 1024)]
            remote(buf, kept, ls.at[3], ll.at[0], at_x(turn, j // (LCH // 2))).start()

            @pl.when(jnp.logical_not(src_l) & (j >= LCH // 2))
            def _():
                remote(buf, buf, ls.at[4], lq.at[0], partner).start()

    def answered(place):
        @pl.when(hub & (n_down > place))
        def _():
            pl.semaphore_wait(ready.at[place], 1)

    def columns():
        @pl.when(src_l)
        def _():
            pl.loop(0, LCH // 2)(lambda j: column(j, (2, 3)))
            theirs = L.at[pl.ds(512, 512)]
            remote(theirs, theirs, lq.at[0], lq.at[0], partner).wait_recv()
            pl.loop(LCH // 2, LCH)(lambda j: column(j, (2, 3)))
            for slot in range(2):
                answered(slot)
                pl.loop(0, LCH)(lambda j: column(j, (slot,)))

        @pl.when(jnp.logical_not(src_l))
        def _():
            for place in range(3):
                answered(place)
            pl.loop(0, LCH)(lambda j: column(j, (0, 1, 2, 3)))

    def corner(j):
        buf = X.at[hb, rows_of(j)]

        @pl.when(z == 0)
        def _():
            X[hb, rows_of(j)] = U[hb, rows_of(j), 0:NB]

        @pl.when(z != 0)
        def _():
            remote(buf, buf, xr.at[j], xr.at[j], partner).wait_recv()

        for slot, (cond, device) in enumerate(plane_x):
            pl.when(cond)(remote(buf, buf, xs.at[slot], xr.at[j], device).start)
        for slot, off in enumerate((2, 1, -1)):
            remote(buf, buf, xs.at[3 + slot], xl.at[hb], at_x(off, 0)).start()

    def lower_rows(which, base):
        @pl.when(which == 0)
        def _():
            for part in range(2):
                raw = L[pl.ds(pl.multiple_of(base + part * NB, NB), NB)]
                value = dot(raw, W[2, 0]) + dot(raw, W[2, 1])
                LF[part * NB : (part + 1) * NB, 0:NB] = jnp.where(part * 16 + r > 0, value, 0.0).astype(BF16)

        @pl.when(which == 1)
        def _():
            for part in range(2):
                raw = L[pl.ds(pl.multiple_of(base + part * NB, NB), NB)]
                D1[part * NB : (part + 1) * NB] = dot(raw, W[3, 0]) + dot(raw, W[3, 1])

    def lower():
        @pl.when((core == 1) & jnp.logical_not(src_l))
        def _():
            remote(L.at[mine], L.at[mine], lq.at[0], lq.at[0], partner).wait_recv()

        lower_rows(fb, core * 512)
        kept = L.at[pl.ds(1024, 512)]
        remote(kept, kept, ll.at[0], ll.at[0], partner).wait_recv()
        lower_rows(1 - fb, 1024)

    def corners():
        @pl.when(first_core)
        def _():
            for k in range(2):

                @pl.when(x != 1 - k)
                def _():
                    remote(X.at[k], X.at[k], xl.at[k], xl.at[k], partner).wait_recv()

            remote(X, X, xs.at[6], xq.at[0], partner).start()

        @pl.when(core == 1)
        def _():
            remote(X, X, xq.at[0], xq.at[0], partner).wait_recv()

        l10 = (dot(X[1], W[2, 0]) + dot(X[1], W[2, 1])).astype(BF16)
        u01 = (dot(W[0, 0], X[0]) + dot(W[0, 1], X[0])).astype(BF16)
        small[0] = (dot(W[1, 0], l10) + dot(W[1, 1], l10)).astype(BF16)
        small[1] = (dot(u01, W[3, 0]) + dot(u01, W[3, 1])).astype(BF16)
        small[2] = u01
        for part in range(2):
            rows = pl.ds(part * NB, NB)
            at = part * 16 + r
            lower0 = LF[rows, 0:NB]
            lower1 = D1[rows] - dot(lower0, small[1])
            lower1 = jnp.where(at > 1, lower1, 0.0).astype(BF16)

            @pl.when((c == 0) & (at > 0))
            def _():
                M[rows, 0:NB] = lower0

            @pl.when((c == 1) & (at > 1))
            def _():
                M[rows, 0:NB] = lower1

            if part == 0:

                @pl.when((c == 1) & (r == 1))
                def _():
                    M[rows, 0:NB] = (M[rows, 0:NB].astype(F32) - dot(lower0, small[2])).astype(BF16)

            LF[rows, 0:NB] = (lower0.astype(F32) - dot(lower1, small[0])).astype(BF16)
            LF[rows, NB : 2 * NB] = lower1

    def steps(begin, end):
        @pl.loop(begin, end)
        def _(it):
            for start, rate, count, handle in on_1:
                k = it - start

                @pl.when((k >= 0) & (k < count))
                def _(k=k, rate=rate, handle=handle):
                    for i in range(rate):
                        handle(k * rate + i)

    @pl.when(first_core)
    def _():
        early = (y == 0) & (z != 0)
        had = jnp.where(src_l, hb, -1)

        def near_blocks():
            pl.loop(jnp.where(had == near_side, 1, 0), SHARED)(lambda q: take_and_give(near_side, q))

        def far_blocks():
            @pl.loop(SHARED, 7)
            def _(q):
                take(0, q)
                take(1, q)

            pl.loop(jnp.where(had == 1 - near_side, 1, 0), SHARED)(lambda q: take(1 - near_side, q))

        @pl.when(early)
        def _():
            near_blocks()
            far_blocks()

        columns()
        pl.when(had == near_side)(lambda: take_and_give(near_side, 0))
        pl.when(had == 1 - near_side)(lambda: take(1 - near_side, 0))

        @pl.when(hub)
        def _():
            pl.loop(0, XCH)(corner)

        lower()
        pl.when(jnp.logical_not(early))(near_blocks)
        corners()
        pl.when(jnp.logical_not(early))(far_blocks)

        for g, (tree, first, count, _, _, _) in enumerate(GROUPS):
            buf = U.at[0, :, pl.ds(first * 64, count * 64)]
            for slot, cond, device in children[0][g]:
                pl.when(cond & (y == 0))(remote(buf, buf, us.at[0, g, slot], ur.at[0, 0], device).wait_send)
        pl.when(y == 0)(remote(U.at[0], U.at[0], ps.at[0], pr.at[0, 0], partner).wait_send)
        shared = UF.at[0:NB, pl.ds(0, SHARED * NB)]
        remote(shared, shared, fs.at[0], fr.at[0], partner).wait_send()
        whole = L.at[pl.ds(0, 1024)]
        for slot, (cond, device) in enumerate(plane):
            pl.when(cond)(remote(whole, whole, ls.at[slot], lr.at[0], device).wait_send)
        remote(whole, whole, ls.at[3], ll.at[0], partner).wait_send()
        part = L.at[pl.ds(512, 512)]
        pl.when(jnp.logical_not(src_l))(remote(part, part, ls.at[4], lq.at[0], partner).wait_send)

        @pl.when(hub)
        def _():
            for slot, (cond, device) in enumerate(plane_x):
                pl.when(cond)(remote(X.at[0], X.at[0], xs.at[slot], xr.at[0], device).wait_send)
            for slot in range(3):
                remote(X.at[0], X.at[0], xs.at[3 + slot], xl.at[0], partner).wait_send()

        remote(X, X, xs.at[6], xq.at[0], partner).wait_send()

    @pl.when(core == 1)
    def _():
        mine_1 = L.at[pl.ds(512, 512)]
        give = remote(mine_1, mine_1, ls.at[4], lq.at[0], partner)
        pl.when(src_l)(give.start)
        lower_at, corners_at = lut(y, LOWER_AT), lut(y, CORNERS_AT)

        @pl.when(y == 0)
        def _():
            @pl.loop(0, 7)
            def _(q):
                raw = U[1, :, block(q)]
                value = dot(W[1, 0], raw) + dot(W[1, 1], raw)
                B1[:, block(q)] = value

                UF[NB : 2 * NB, block(q)] = jnp.where((q > 0) | (c > 1), value, 0.0).astype(BF16)

            remote(U.at[0], U.at[0], pr.at[0, 0], pr.at[0, 0], partner).wait_recv()
            pl.loop(SHARED, 7)(lambda q: panel(0, q))

        pl.when(y != 0)(lambda: steps(0, lower_at))
        lower()
        pl.when(y != 0)(lambda: steps(lower_at, corners_at))
        corners()
        pl.when(y != 0)(lambda: steps(corners_at, STEPS))
        shared = UF.at[0:NB, pl.ds(0, SHARED * NB)]
        remote(shared, shared, fr.at[0], fr.at[0], partner).wait_recv()

        @pl.when(y == 0)
        def _():
            LF[0:NB] = jnp.zeros((NB, 2 * NB), BF16)

            @pl.loop(0, COLS // NB)
            def _(q):
                cols = block(q)

                @pl.when((q > 0) | (c > 1))
                def _():
                    M[0:NB, cols] = (B1[:, cols] - dot(small[0], UF[0:NB, cols])).astype(BF16)

        for side in range(2):
            for g, (tree, first, count, _, _, _) in enumerate(GROUPS):
                buf = U.at[side, :, pl.ds(first * 64, count * 64)]
                for slot, cond, device in children[side][g]:
                    sent = cond if side == 1 else cond & (y != 0)
                    pl.when(sent)(remote(buf, buf, us.at[side, g, slot], ur.at[side, 0], device).wait_send)
            sent = remote(U.at[side], U.at[side], ps.at[side], pr.at[side, 0], partner)
            if side == 1:
                sent.wait_send()
            else:
                pl.when(y != 0)(sent.wait_send)
        pl.when(src_l)(give.wait_send)


def update(UF, LF, M, out, O, sems):
    copies = []
    for q in range(COLS // NB):
        cols = pl.ds(q * NB, NB)
        O[:, cols] = (M[:, cols].astype(F32) - dot(LF[...], UF[:, cols])).astype(BF16)
        copies.append(pltpu.make_async_copy(O.at[:, cols], out.at[:, cols], sems.at[q]))
        copies[-1].start()
    for copy in copies:
        copy.wait()


def body(matrix, lower_inv, upper_inv):
    D = pltpu.SemaphoreType.DMA
    vmem = pl.BlockSpec(memory_space=pltpu.VMEM)
    hbm = pl.BlockSpec(memory_space=pltpu.HBM)
    UF, LF, M = pl.pallas_call(
        gather,
        out_shape=(
            jax.ShapeDtypeStruct((2 * NB, COLS), BF16),
            jax.ShapeDtypeStruct((512, 2 * NB), BF16),
            jax.ShapeDtypeStruct((512, COLS), BF16),
        ),
        in_specs=[hbm] * 3,
        out_specs=(vmem, vmem, vmem),
        scratch_shapes=[
            pltpu.VMEM((2, NB, COLS), BF16),
            pltpu.VMEM((2, NB, NB), BF16),
            pltpu.VMEM((1536, NB), BF16),
            pltpu.VMEM((2, 2, NB, NB), F32),
            pltpu.VMEM((4, 2, NB, NB), BF16),
            pltpu.VMEM((3, NB, NB), BF16),
            pltpu.VMEM((512, NB), F32),
            D((2, 3, 2)),
            D((2, UCH)),
            D((2,)),
            D((2, 7)),
            D((1,)),
            D((1,)),
            D((5,)),
            D((LCH,)),
            D((1,)),
            D((1,)),
            D((7,)),
            D((XCH,)),
            D((2,)),
            D((1,)),
            pltpu.VMEM((NB, COLS), F32),
            pltpu.SemaphoreType.REGULAR((3,)),
            pltpu.SemaphoreType.REGULAR,
            D((5,)),
        ],
        compiler_params=pltpu.CompilerParams(
            collective_id=0, has_side_effects=True, vmem_limit_bytes=32 * 2**20
        ),
    )(*(pltpu.with_memory_space_constraint(a, pltpu.HBM) for a in (matrix, lower_inv, upper_inv)))
    return pl.pallas_call(
        update,
        out_shape=jax.ShapeDtypeStruct(matrix.shape, matrix.dtype),
        in_specs=[vmem] * 3,
        out_specs=hbm,
        scratch_shapes=[pltpu.VMEM((512, COLS), BF16), D((COLS // NB,))],
        compiler_params=pltpu.CompilerParams(vmem_limit_bytes=16 * 2**20),
    )(UF, LF, M)


def solution(mesh):
    in_specs = (P("row", "col"), P(), P())
    return jax.shard_map(body, mesh=mesh, in_specs=in_specs, out_specs=P("row", "col"), check_vma=False)
```

```python
import jax
import jax.numpy as jnp
from jax import lax
from jax.experimental import pallas as pl
from jax.experimental.pallas import tpu as pltpu
from jax.sharding import PartitionSpec as P

MESH = pl.DeviceIdType.MESH
F32 = jnp.float32
BF16 = jnp.bfloat16
NB = 256
COLS = 1792
NY, NZ, NX = 8, 8, 4

NEAR = {0: (1, 7), 1: (2,), 2: (3,), 3: (4,), 7: (6,), 6: (5,)}
FAR = {0: (2, 6), 2: (1, 3), 3: (4,), 6: (7, 5)}
WIDE = {0: (2, 6), 2: (4, 3, 1), 6: (5, 7)}
LONG = {0: (2,), 2: (3, 1), 3: (4,), 4: (5,), 5: (6,), 6: (7,)}

GROUPS = (
    (LONG, 0, 4, 0, 1, (0, 16, 10, 16, 22, 30, 36, 42)),
    (LONG, 4, 16, 4, 1, (0, 16, 10, 16, 22, 30, 36, 42)),
    (NEAR, 20, 8, 20, 2, (0, 8, 14, 20, 28, 20, 14, 8)),
)
FIRST = (FAR, (0, 16, 10, 16, 22, 16, 10, 16))
UCH = 28
SHARED = 5
LROWS = 64
LCH = 1024 // LROWS
XCH = NB // LROWS
STEPS = 72
LOWER_AT = (56, 48, 56, 56, 46, 56, 56, 48)
CORNERS_AT = (62, 56, 62, 62, 56, 62, 62, 56)
PLANE = (0, 10, 6, 10, 15, 10, 6, 10)
FROM_HUB = (0, 5, 10, 6)
PLANE_X = (0, 10, 6, 10, 11, 9, 6, 9)


def offsets(tree, slot):
    out = []
    for k in range(8):
        children = tree.get(k, ())
        out.append((children[slot] - k + 4) % 8 - 4 if slot < len(children) else 0)
    return out


def lut(index, values):
    result = jnp.int32(values[0])
    for k in range(1, len(values)):
        if values[k] != values[0]:
            result = jnp.where(index == k, jnp.int32(values[k]), result)
    return result


def split(value):
    high = value.astype(BF16)
    return high, (value - high.astype(F32)).astype(BF16)


def dot(a, b):
    return jnp.dot(a, b, preferred_element_type=F32)


def remote(src, dst, send, recv, device):
    return pltpu.make_async_remote_copy(
        src_ref=src, dst_ref=dst, send_sem=send, recv_sem=recv, device_id=device, device_id_type=MESH
    )


def gather(
    mat, linv, uinv, UF, LF, M, U, X, L, inv, W, small, D1, us, ur, ps, pr, fs, fr, ls, lr, ll, lq, xs, xr, xl, xq, B1, ready, answer, loc
):
    r = lax.axis_index("row")
    c = lax.axis_index("col")
    y, core = r // 2, lax.rem(r, 2)
    z, x = c // NX, lax.rem(c, NX)
    partner = (y * 2 + 1 - core, c)
    first_core = core == 0
    hub = x < 2
    fb = jnp.where((x == 1) | (x == 2), 1, 0)
    hb = jnp.where(x == 0, 1, 0)
    turn = jnp.where(lax.rem(x, 2) == 0, 1, -1)
    src_l = c < 2

    def at_y(off, to_core):
        return (lax.rem(y + off + NY, NY) * 2 + to_core, c)

    def at_z(off):
        return (r, lax.rem(z + off + NZ, NZ) * NX + x)

    def at_x(off, to_core):
        return (y * 2 + to_core, z * NX + lax.rem(x + off + NX, NX))

    def u_part(ref, j):
        col = pl.multiple_of(j // 2 * 128, 128)
        row = pl.multiple_of(lax.rem(j, 2) * 128, 128)
        return ref.at[pl.ds(row, 128), pl.ds(col, 128)]

    def block(q):
        return pl.ds(pl.multiple_of(q * NB, NB), NB)

    barrier = pltpu.get_barrier_semaphore()

    def greet(device):
        pl.semaphore_signal(barrier, inc=1, device_id=device, device_id_type=MESH)

    z_links = [(k, child) for k in range(NZ) for child in sorted(set(FAR.get(k, ())) | set(WIDE.get(k, ())))]
    down = [[child - k for k, child in z_links if k == at] for at in range(NZ)]
    up = [[k - child for k, child in z_links if child == at] for at in range(NZ)]
    z_down = [lut(z, [(d[i] + 4) % 8 - 4 if i < len(d) else 0 for d in down]) for i in range(max(map(len, down)))]
    z_up = [lut(z, [(d[i] + 4) % 8 - 4 if i < len(d) else 0 for d in up]) for i in range(max(map(len, up)))]
    n_down = lut(z, [len(d) for d in down])
    n_up = lut(z, [len(d) for d in up])
    rank = [[down[(at + off) % NZ].index(-off) for off in d] for at, d in enumerate(up)]
    z_rank = [lut(z, [k[i] if i < len(k) else 0 for k in rank]) for i in range(len(z_up))]

    @pl.when(core == 1)
    def _():
        for off in (1, -1, 2, -2):
            greet(at_y(off, 1))
        pl.when((y == 1) | (y == 2) | (y == 6) | (y == 7))(lambda: greet((0, c)))

    pl.when(core == 1)(lambda: greet(partner))
    greet(at_x(turn, 0))

    @pl.when(first_core)
    def _():
        pl.when(x != 0)(lambda: greet(at_x(-x, 0)))
        pl.when(x != 1)(lambda: greet(at_x(1 - x, 0)))
        pl.when(x >= 2)(lambda: greet(at_x(-turn, 0)))
        for off in z_down:
            pl.when(hub & (off != 0))(lambda off=off: greet(at_z(off)))

    local = [
        pltpu.make_async_copy(linv, inv.at[0], loc.at[1]),
        pltpu.make_async_copy(uinv, inv.at[1], loc.at[2]),
        pltpu.make_async_copy(mat, M, loc.at[0]),
    ]
    mine = pl.ds(pl.multiple_of(core * 512, 512), 512)
    own_rows = pltpu.make_async_copy(mat.at[pl.ds(0, NB)], U.at[core], loc.at[3])
    own_cols = pltpu.make_async_copy(mat.at[:, pl.ds(0, NB)], L.at[mine], loc.at[4])
    local[0].start()
    local[1].start()
    pl.when(y == 0)(own_rows.start)
    pl.when(src_l)(own_cols.start)
    local[2].start()
    count_0 = 3 + jnp.where(hub, 4 + n_up, 0) + jnp.where(y == 0, 4, 0)
    pl.semaphore_wait(barrier, jnp.where(first_core, count_0, 4))

    @pl.when(first_core)
    def _():
        pl.semaphore_signal(answer, inc=1, device_id=partner, device_id_type=MESH)


    near_side = jnp.where(y <= 4, 0, 1)
    positions = (y, lax.rem(NY - y, NY))
    def u_children(side, g):
        out = []
        for slot in range(2):
            offs = offsets(GROUPS[g][0], slot)
            fast = offsets(FIRST[0], slot) if g == 0 else offs
            if any(offs) or any(fast):
                off = lut(positions[side], offs)
                if g == 0:
                    off = jnp.where(c == 1 - side, lut(positions[side], fast), off)
                out.append((slot, off != 0, at_y(off if side == 0 else -off, 1)))
        return out

    children = [[u_children(side, g) for g in range(len(GROUPS))] for side in range(2)]


    @pl.when(y == 0)
    def _():
        for side in range(2):

            @pl.when(core == side)
            def _(side=side):
                for g, (tree, first, count, _, _, _) in enumerate(GROUPS):

                    @pl.loop(first, first + count)
                    def _(j, g=g):
                        for slot, cond, device in children[side][g]:
                            there = u_part(U.at[side], j)
                            copy = remote(u_part(mat, j), there, us.at[side, g, slot], ur.at[side, j], device)
                            pl.when(cond)(copy.start)

                if side == 1:
                    pl.semaphore_wait(answer, 1)

                    @pl.loop(0, 7)
                    def _(q):
                        raw = mat.at[pl.ds(0, NB), block(q)]
                        remote(raw, U.at[1, :, block(q)], ps.at[1], pr.at[1, q], partner).start()

                else:
                    remote(mat.at[pl.ds(0, NB)], U.at[0], ps.at[0], pr.at[0, 0], partner).start()

    for off, place in zip(z_up, z_rank):

        @pl.when(first_core & hub & (off != 0))
        def _(off=off, place=place):
            pl.semaphore_signal(ready.at[place], inc=1, device_id=at_z(off), device_id_type=MESH)

    local[0].wait()
    local[1].wait()
    for k in range(4):
        high, low = split(inv[k // 2, k % 2])
        W[k, 0] = high
        W[k, 1] = low
    pl.when(y == 0)(own_rows.wait)
    pl.when(src_l)(own_cols.wait)
    local[2].wait()

    @pl.when((core == 1) & (y != 0))
    def _():
        pl.semaphore_wait(answer, 1)

    def panel(side, q):
        cols = block(q)
        raw = U[side, :, cols]
        value = dot(W[side, 0], raw) + dot(W[side, 1], raw)
        UF[block(side), cols] = jnp.where((q > 0) | (c > 1), value, 0.0).astype(BF16)

        @pl.when((r == 0) & (side == 0) & ((q > 0) | (c > 0)))
        def _():
            M[0:NB, cols] = value.astype(BF16)

    def hand_on(side, g, first, tree):
        def event(j):
            j = j + first
            buf = u_part(U.at[side], j)
            remote(buf, buf, ur.at[side, j], ur.at[side, j], partner).wait_recv()
            for slot, cond, device in children[side][g]:
                pl.when(cond)(remote(buf, buf, us.at[side, g, slot], ur.at[side, j], device).start)

            @pl.when(lax.rem(j, 4) == 3)
            def _():
                q = j // 4
                raw = U.at[side, :, block(q)]
                remote(raw, raw, ps.at[side], pr.at[side, q], partner).start()
                if first >= 4 * SHARED:
                    panel(side, q)
                else:
                    pl.when(side != near_side)(lambda: panel(side, q))

        return event

    def take(side, q):
        @pl.when((y != 0) | (side == 1))
        def _():
            raw = U.at[side, :, block(q)]
            remote(raw, raw, pr.at[side, q], pr.at[side, q], partner).wait_recv()

        panel(side, q)

    def take_and_give(side, q):
        take(side, q)
        done = UF.at[block(side), block(q)]
        remote(done, done, fs.at[0], fr.at[0], partner).start()

    on_1 = []
    for side in range(2):
        for g, (tree, first, count, start, stride, arrival) in enumerate(GROUPS):
            at = lut(positions[side], arrival)
            if g == 0:
                at = jnp.where(c == 1 - side, lut(positions[side], FIRST[1]), at)
            on_1.append((start + at, stride, count, hand_on(side, g, first, tree)))

    def rows_of(j, base=0):
        return pl.ds(pl.multiple_of(base + j * LROWS, LROWS), LROWS)

    plane = []
    for slot in range(2):
        off = lut(z, offsets(FAR, slot))
        plane.append((hub & (off != 0), at_z(off)))
    plane.append((hub, at_x(-turn, 0)))
    plane_x = []
    for slot in range(3):
        off = lut(z, offsets(WIDE, slot))
        plane_x.append((off != 0, at_z(off)))

    def from_hub(side):
        return jnp.where(side == 0, x, lax.rem(1 - x + NX, NX))

    def column(j, slots):
        buf = L.at[rows_of(j)]

        @pl.when(jnp.logical_not(src_l))
        def _():
            remote(buf, buf, lr.at[j], lr.at[j], partner).wait_recv()

        for slot, (cond, device) in enumerate(plane):
            if slot in slots:
                pl.when(cond)(remote(buf, buf, ls.at[slot], lr.at[j], device).start)
        if 3 in slots:
            kept = L.at[rows_of(lax.rem(j, LCH // 2), 1024)]
            remote(buf, kept, ls.at[3], ll.at[0], at_x(turn, j // (LCH // 2))).start()

            @pl.when(jnp.logical_not(src_l) & (j >= LCH // 2))
            def _():
                remote(buf, buf, ls.at[4], lq.at[0], partner).start()

    def answered(place):
        @pl.when(hub & (n_down > place))
        def _():
            pl.semaphore_wait(ready.at[place], 1)

    def columns():
        @pl.when(src_l)
        def _():
            pl.loop(0, LCH // 2)(lambda j: column(j, (2, 3)))
            theirs = L.at[pl.ds(512, 512)]
            remote(theirs, theirs, lq.at[0], lq.at[0], partner).wait_recv()
            pl.loop(LCH // 2, LCH)(lambda j: column(j, (2, 3)))
            for slot in range(2):
                answered(slot)
                pl.loop(0, LCH)(lambda j: column(j, (slot,)))

        @pl.when(jnp.logical_not(src_l))
        def _():
            for place in range(3):
                answered(place)
            pl.loop(0, LCH)(lambda j: column(j, (0, 1, 2, 3)))

    def corner(j):
        buf = X.at[hb, rows_of(j)]

        @pl.when(z == 0)
        def _():
            X[hb, rows_of(j)] = U[hb, rows_of(j), 0:NB]

        @pl.when(z != 0)
        def _():
            remote(buf, buf, xr.at[j], xr.at[j], partner).wait_recv()

        for slot, (cond, device) in enumerate(plane_x):
            pl.when(cond)(remote(buf, buf, xs.at[slot], xr.at[j], device).start)
        for slot, off in enumerate((2, 1, -1)):
            remote(buf, buf, xs.at[3 + slot], xl.at[hb], at_x(off, 0)).start()

    def lower_rows(which, base):
        @pl.when(which == 0)
        def _():
            for part in range(2):
                raw = L[pl.ds(pl.multiple_of(base + part * NB, NB), NB)]
                value = dot(raw, W[2, 0]) + dot(raw, W[2, 1])
                LF[part * NB : (part + 1) * NB, 0:NB] = jnp.where(part * 16 + r > 0, value, 0.0).astype(BF16)

        @pl.when(which == 1)
        def _():
            for part in range(2):
                raw = L[pl.ds(pl.multiple_of(base + part * NB, NB), NB)]
                D1[part * NB : (part + 1) * NB] = dot(raw, W[3, 0]) + dot(raw, W[3, 1])

    def lower():
        @pl.when((core == 1) & jnp.logical_not(src_l))
        def _():
            remote(L.at[mine], L.at[mine], lq.at[0], lq.at[0], partner).wait_recv()

        lower_rows(fb, core * 512)
        kept = L.at[pl.ds(1024, 512)]
        remote(kept, kept, ll.at[0], ll.at[0], partner).wait_recv()
        lower_rows(1 - fb, 1024)

    def corners():
        @pl.when(first_core)
        def _():
            for k in range(2):

                @pl.when(x != 1 - k)
                def _():
                    remote(X.at[k], X.at[k], xl.at[k], xl.at[k], partner).wait_recv()

            remote(X, X, xs.at[6], xq.at[0], partner).start()

        @pl.when(core == 1)
        def _():
            remote(X, X, xq.at[0], xq.at[0], partner).wait_recv()

        l10 = (dot(X[1], W[2, 0]) + dot(X[1], W[2, 1])).astype(BF16)
        u01 = (dot(W[0, 0], X[0]) + dot(W[0, 1], X[0])).astype(BF16)
        small[0] = (dot(W[1, 0], l10) + dot(W[1, 1], l10)).astype(BF16)
        small[1] = (dot(u01, W[3, 0]) + dot(u01, W[3, 1])).astype(BF16)
        small[2] = u01
        for part in range(2):
            rows = pl.ds(part * NB, NB)
            at = part * 16 + r
            lower0 = LF[rows, 0:NB]
            lower1 = D1[rows] - dot(lower0, small[1])
            lower1 = jnp.where(at > 1, lower1, 0.0).astype(BF16)

            @pl.when((c == 0) & (at > 0))
            def _():
                M[rows, 0:NB] = lower0

            @pl.when((c == 1) & (at > 1))
            def _():
                M[rows, 0:NB] = lower1

            if part == 0:

                @pl.when((c == 1) & (r == 1))
                def _():
                    M[rows, 0:NB] = (M[rows, 0:NB].astype(F32) - dot(lower0, small[2])).astype(BF16)

            LF[rows, 0:NB] = (lower0.astype(F32) - dot(lower1, small[0])).astype(BF16)
            LF[rows, NB : 2 * NB] = lower1

    def steps(begin, end):
        @pl.loop(begin, end)
        def _(it):
            for start, stride, count, handle in on_1:
                k = it - start
                ok = (k >= 0) & (k < count * stride)
                if stride == 2:
                    ok = ok & (lax.rem(k, 2) == 0)

                @pl.when(ok)
                def _(k=k, stride=stride, handle=handle):
                    handle(k // stride if stride > 1 else k)

    @pl.when(first_core)
    def _():
        early = (y == 0) & (z != 0)
        had = jnp.where(src_l, hb, -1)

        def near_blocks():
            pl.loop(jnp.where(had == near_side, 1, 0), SHARED)(lambda q: take_and_give(near_side, q))

        def last_blocks():
            @pl.loop(SHARED, 7)
            def _(q):
                take(0, q)
                take(1, q)

        def far_blocks():
            middle = (y >= 3) & (y <= 5)
            pl.when(jnp.logical_not(middle))(last_blocks)
            pl.loop(jnp.where(had == 1 - near_side, 1, 0), SHARED)(lambda q: take(1 - near_side, q))
            pl.when(middle)(last_blocks)

        @pl.when(early)
        def _():
            near_blocks()
            far_blocks()

        columns()
        pl.when(had == near_side)(lambda: take_and_give(near_side, 0))
        pl.when(had == 1 - near_side)(lambda: take(1 - near_side, 0))

        @pl.when(hub)
        def _():
            pl.loop(0, XCH)(corner)

        lower()
        pl.when(jnp.logical_not(early))(near_blocks)
        corners()
        pl.when(jnp.logical_not(early))(far_blocks)

        for g, (tree, first, count, _, _, _) in enumerate(GROUPS):
            buf = U.at[0, :, pl.ds(first * 64, count * 64)]
            for slot, cond, device in children[0][g]:
                pl.when(cond & (y == 0))(remote(buf, buf, us.at[0, g, slot], ur.at[0, 0], device).wait_send)
        pl.when(y == 0)(remote(U.at[0], U.at[0], ps.at[0], pr.at[0, 0], partner).wait_send)
        shared = UF.at[0:NB, pl.ds(0, SHARED * NB)]
        remote(shared, shared, fs.at[0], fr.at[0], partner).wait_send()
        whole = L.at[pl.ds(0, 1024)]
        for slot, (cond, device) in enumerate(plane):
            pl.when(cond)(remote(whole, whole, ls.at[slot], lr.at[0], device).wait_send)
        remote(whole, whole, ls.at[3], ll.at[0], partner).wait_send()
        part = L.at[pl.ds(512, 512)]
        pl.when(jnp.logical_not(src_l))(remote(part, part, ls.at[4], lq.at[0], partner).wait_send)

        @pl.when(hub)
        def _():
            for slot, (cond, device) in enumerate(plane_x):
                pl.when(cond)(remote(X.at[0], X.at[0], xs.at[slot], xr.at[0], device).wait_send)
            for slot in range(3):
                remote(X.at[0], X.at[0], xs.at[3 + slot], xl.at[0], partner).wait_send()

        remote(X, X, xs.at[6], xq.at[0], partner).wait_send()

    @pl.when(core == 1)
    def _():
        mine_1 = L.at[pl.ds(512, 512)]
        give = remote(mine_1, mine_1, ls.at[4], lq.at[0], partner)
        pl.when(src_l)(give.start)
        lower_at, corners_at = lut(y, LOWER_AT), lut(y, CORNERS_AT)

        @pl.when(y == 0)
        def _():
            @pl.loop(0, 7)
            def _(q):
                raw = U[1, :, block(q)]
                value = dot(W[1, 0], raw) + dot(W[1, 1], raw)
                B1[:, block(q)] = value

                UF[NB : 2 * NB, block(q)] = jnp.where((q > 0) | (c > 1), value, 0.0).astype(BF16)

            remote(U.at[0], U.at[0], pr.at[0, 0], pr.at[0, 0], partner).wait_recv()
            pl.loop(SHARED, 7)(lambda q: panel(0, q))

        pl.when(y != 0)(lambda: steps(0, lower_at))
        lower()
        pl.when(y != 0)(lambda: steps(lower_at, corners_at))
        corners()
        pl.when(y != 0)(lambda: steps(corners_at, STEPS))
        shared = UF.at[0:NB, pl.ds(0, SHARED * NB)]
        remote(shared, shared, fr.at[0], fr.at[0], partner).wait_recv()

        @pl.when(y == 0)
        def _():
            LF[0:NB] = jnp.zeros((NB, 2 * NB), BF16)

            @pl.loop(0, COLS // NB)
            def _(q):
                cols = block(q)

                @pl.when((q > 0) | (c > 1))
                def _():
                    M[0:NB, cols] = (B1[:, cols] - dot(small[0], UF[0:NB, cols])).astype(BF16)

        for side in range(2):
            for g, (tree, first, count, _, _, _) in enumerate(GROUPS):
                buf = U.at[side, :, pl.ds(first * 64, count * 64)]
                for slot, cond, device in children[side][g]:
                    sent = cond if side == 1 else cond & (y != 0)
                    pl.when(sent)(remote(buf, buf, us.at[side, g, slot], ur.at[side, 0], device).wait_send)
            sent = remote(U.at[side], U.at[side], ps.at[side], pr.at[side, 0], partner)
            if side == 1:
                sent.wait_send()
            else:
                pl.when(y != 0)(sent.wait_send)
        pl.when(src_l)(give.wait_send)


def update(UF, LF, M, out, O, sems):
    copies = []
    for q in range(COLS // NB):
        cols = pl.ds(q * NB, NB)
        O[:, cols] = (M[:, cols].astype(F32) - dot(LF[...], UF[:, cols])).astype(BF16)
        copies.append(pltpu.make_async_copy(O.at[:, cols], out.at[:, cols], sems.at[q]))
        copies[-1].start()
    for copy in copies:
        copy.wait()


def body(matrix, lower_inv, upper_inv):
    D = pltpu.SemaphoreType.DMA
    vmem = pl.BlockSpec(memory_space=pltpu.VMEM)
    hbm = pl.BlockSpec(memory_space=pltpu.HBM)
    UF, LF, M = pl.pallas_call(
        gather,
        out_shape=(
            jax.ShapeDtypeStruct((2 * NB, COLS), BF16),
            jax.ShapeDtypeStruct((512, 2 * NB), BF16),
            jax.ShapeDtypeStruct((512, COLS), BF16),
        ),
        in_specs=[hbm] * 3,
        out_specs=(vmem, vmem, vmem),
        scratch_shapes=[
            pltpu.VMEM((2, NB, COLS), BF16),
            pltpu.VMEM((2, NB, NB), BF16),
            pltpu.VMEM((1536, NB), BF16),
            pltpu.VMEM((2, 2, NB, NB), F32),
            pltpu.VMEM((4, 2, NB, NB), BF16),
            pltpu.VMEM((3, NB, NB), BF16),
            pltpu.VMEM((512, NB), F32),
            D((2, 3, 2)),
            D((2, UCH)),
            D((2,)),
            D((2, 7)),
            D((1,)),
            D((1,)),
            D((5,)),
            D((LCH,)),
            D((1,)),
            D((1,)),
            D((7,)),
            D((XCH,)),
            D((2,)),
            D((1,)),
            pltpu.VMEM((NB, COLS), F32),
            pltpu.SemaphoreType.REGULAR((3,)),
            pltpu.SemaphoreType.REGULAR,
            D((5,)),
        ],
        compiler_params=pltpu.CompilerParams(
            collective_id=0, has_side_effects=True, vmem_limit_bytes=32 * 2**20
        ),
    )(*(pltpu.with_memory_space_constraint(a, pltpu.HBM) for a in (matrix, lower_inv, upper_inv)))
    return pl.pallas_call(
        update,
        out_shape=jax.ShapeDtypeStruct(matrix.shape, matrix.dtype),
        in_specs=[vmem] * 3,
        out_specs=hbm,
        scratch_shapes=[pltpu.VMEM((512, COLS), BF16), D((COLS // NB,))],
        compiler_params=pltpu.CompilerParams(vmem_limit_bytes=16 * 2**20),
    )(UF, LF, M)


def solution(mesh):
    in_specs = (P("row", "col"), P(), P())
    return jax.shard_map(body, mesh=mesh, in_specs=in_specs, out_specs=P("row", "col"), check_vma=False)
```

```python
import jax
import jax.numpy as jnp
from jax import lax
from jax.experimental import pallas as pl
from jax.experimental.pallas import tpu as pltpu
from jax.sharding import PartitionSpec as P

MESH = pl.DeviceIdType.MESH
F32 = jnp.float32
BF16 = jnp.bfloat16
NB = 256
COLS = 1792
NY, NZ, NX = 8, 8, 4

NEAR = {0: (1, 7), 1: (2,), 2: (3,), 3: (4,), 7: (6,), 6: (5,)}
FAR = {0: (2, 6), 2: (1, 3), 3: (4,), 6: (7, 5)}
WIDE = {0: (2, 6), 2: (4, 3, 1), 6: (5, 7)}
LONG = {0: (2,), 2: (3, 1), 3: (4,), 4: (5,), 5: (6,), 6: (7,)}
SHORT = {k: v for k, v in LONG.items() if k < 6}

GROUPS = (
    (LONG, 0, 4, 0, 1, (0, 16, 10, 16, 22, 30, 36, 42)),
    (LONG, 4, 16, 4, 1, (0, 16, 10, 16, 22, 30, 36, 42)),
    (NEAR, 20, 8, 20, 2, (0, 8, 14, 20, 28, 20, 14, 8)),
)
FIRST = (FAR, (0, 16, 10, 16, 22, 16, 10, 16))
UCH = 28
SHARED = 5
LROWS = 64
LCH = 1024 // LROWS
XCH = NB // LROWS
STEPS = 72
LOWER_AT = (56, 48, 56, 56, 46, 56, 56, 48)
CORNERS_AT = (62, 56, 62, 62, 56, 62, 62, 56)
PLANE = (0, 10, 6, 10, 15, 10, 6, 10)
FROM_HUB = (0, 5, 10, 6)
PLANE_X = (0, 10, 6, 10, 11, 9, 6, 9)


def offsets(tree, slot):
    out = []
    for k in range(8):
        children = tree.get(k, ())
        out.append((children[slot] - k + 4) % 8 - 4 if slot < len(children) else 0)
    return out


def lut(index, values):
    result = jnp.int32(values[0])
    for k in range(1, len(values)):
        if values[k] != values[0]:
            result = jnp.where(index == k, jnp.int32(values[k]), result)
    return result


def split(value):
    high = value.astype(BF16)
    return high, (value - high.astype(F32)).astype(BF16)


def dot(a, b):
    return jnp.dot(a, b, preferred_element_type=F32)


def remote(src, dst, send, recv, device):
    return pltpu.make_async_remote_copy(
        src_ref=src, dst_ref=dst, send_sem=send, recv_sem=recv, device_id=device, device_id_type=MESH
    )


def gather(
    mat, linv, uinv, UF, LF, M, U, X, L, inv, W, small, D1, us, ur, ps, pr, fs, fr, ls, lr, ll, lq, xs, xr, xl, xq, B1, ready, answer, loc
):
    r = lax.axis_index("row")
    c = lax.axis_index("col")
    y, core = r // 2, lax.rem(r, 2)
    z, x = c // NX, lax.rem(c, NX)
    partner = (y * 2 + 1 - core, c)
    first_core = core == 0
    hub = x < 2
    fb = jnp.where((x == 1) | (x == 2), 1, 0)
    hb = jnp.where(x == 0, 1, 0)
    turn = jnp.where(lax.rem(x, 2) == 0, 1, -1)
    src_l = c < 2

    def at_y(off, to_core):
        return (lax.rem(y + off + NY, NY) * 2 + to_core, c)

    def at_z(off):
        return (r, lax.rem(z + off + NZ, NZ) * NX + x)

    def at_x(off, to_core):
        return (y * 2 + to_core, z * NX + lax.rem(x + off + NX, NX))

    def u_part(ref, j):
        col = pl.multiple_of(j // 2 * 128, 128)
        row = pl.multiple_of(lax.rem(j, 2) * 128, 128)
        return ref.at[pl.ds(row, 128), pl.ds(col, 128)]

    def block(q):
        return pl.ds(pl.multiple_of(q * NB, NB), NB)

    barrier = pltpu.get_barrier_semaphore()

    def greet(device):
        pl.semaphore_signal(barrier, inc=1, device_id=device, device_id_type=MESH)

    z_links = [(k, child) for k in range(NZ) for child in sorted(set(FAR.get(k, ())) | set(WIDE.get(k, ())))]
    down = [[child - k for k, child in z_links if k == at] for at in range(NZ)]
    up = [[k - child for k, child in z_links if child == at] for at in range(NZ)]
    z_down = [lut(z, [(d[i] + 4) % 8 - 4 if i < len(d) else 0 for d in down]) for i in range(max(map(len, down)))]
    z_up = [lut(z, [(d[i] + 4) % 8 - 4 if i < len(d) else 0 for d in up]) for i in range(max(map(len, up)))]
    n_down = lut(z, [len(d) for d in down])
    n_up = lut(z, [len(d) for d in up])
    rank = [[down[(at + off) % NZ].index(-off) for off in d] for at, d in enumerate(up)]
    z_rank = [lut(z, [k[i] if i < len(k) else 0 for k in rank]) for i in range(len(z_up))]

    @pl.when(core == 1)
    def _():
        for off in (1, -1, 2, -2):
            greet(at_y(off, 1))
        pl.when((y == 1) | (y == 2) | (y == 6) | (y == 7))(lambda: greet((0, c)))

    pl.when(core == 1)(lambda: greet(partner))
    greet(at_x(turn, 0))

    @pl.when(first_core)
    def _():
        pl.when(x != 0)(lambda: greet(at_x(-x, 0)))
        pl.when(x != 1)(lambda: greet(at_x(1 - x, 0)))
        pl.when(x >= 2)(lambda: greet(at_x(-turn, 0)))
        for off in z_down:
            pl.when(hub & (off != 0))(lambda off=off: greet(at_z(off)))

    local = [
        pltpu.make_async_copy(linv, inv.at[0], loc.at[1]),
        pltpu.make_async_copy(uinv, inv.at[1], loc.at[2]),
        pltpu.make_async_copy(mat, M, loc.at[0]),
    ]
    mine = pl.ds(pl.multiple_of(core * 512, 512), 512)
    own_rows = pltpu.make_async_copy(mat.at[pl.ds(0, NB)], U.at[core], loc.at[3])
    own_cols = pltpu.make_async_copy(mat.at[:, pl.ds(0, NB)], L.at[mine], loc.at[4])
    local[0].start()
    local[1].start()
    pl.when(y == 0)(own_rows.start)
    pl.when(src_l)(own_cols.start)
    local[2].start()
    count_0 = 3 + jnp.where(hub, 4 + n_up, 0) + jnp.where(y == 0, 4, 0)
    pl.semaphore_wait(barrier, jnp.where(first_core, count_0, 4))

    @pl.when(first_core)
    def _():
        pl.semaphore_signal(answer, inc=1, device_id=partner, device_id_type=MESH)


    near_side = jnp.where(y <= 4, 0, 1)
    positions = (y, lax.rem(NY - y, NY))
    def u_children(side, g):
        out = []
        for slot in range(2):
            tree = GROUPS[g][0]
            offs = offsets(SHORT if side == 1 and tree is LONG else tree, slot)
            fast = offsets(FIRST[0], slot) if g == 0 else offs
            if any(offs) or any(fast):
                off = lut(positions[side], offs)
                if g == 0:
                    off = jnp.where(c == 1 - side, lut(positions[side], fast), off)
                out.append((slot, off != 0, at_y(off if side == 0 else -off, 1)))
        return out

    children = [[u_children(side, g) for g in range(len(GROUPS))] for side in range(2)]


    last_groups = [(0, c != 0), (1, c >= 0)]

    def main_sent(side, here):
        for g, (_, first, count, _, _, _) in enumerate(GROUPS):
            buf = U.at[side, :, pl.ds(first * 64, count * 64)]
            for slot, cond, device in children[side][g]:
                pl.when(cond & here)(remote(buf, buf, us.at[side, g, slot], ur.at[side, 0], device).wait_send)

    @pl.when(y == 0)
    def _():
        for side in range(2):

            @pl.when(core == side)
            def _(side=side):
                for g, (tree, first, count, _, _, _) in enumerate(GROUPS):

                    @pl.loop(first, first + count)
                    def _(j, g=g):
                        for slot, cond, device in children[side][g]:
                            there = u_part(U.at[side], j)
                            copy = remote(u_part(mat, j), there, us.at[side, g, slot], ur.at[side, j], device)
                            pl.when(cond)(copy.start)

                if side == 1:
                    pl.semaphore_wait(answer, 1)

                    @pl.loop(0, 7)
                    def _(q):
                        raw = mat.at[pl.ds(0, NB), block(q)]
                        remote(raw, U.at[1, :, block(q)], ps.at[1], pr.at[1, q], partner).start()

                else:
                    remote(mat.at[pl.ds(0, NB)], U.at[0], ps.at[0], pr.at[0, 0], partner).start()

    for off, place in zip(z_up, z_rank):

        @pl.when(first_core & hub & (off != 0))
        def _(off=off, place=place):
            pl.semaphore_signal(ready.at[place], inc=1, device_id=at_z(off), device_id_type=MESH)

    local[0].wait()
    local[1].wait()
    for k in range(4):
        high, low = split(inv[k // 2, k % 2])
        W[k, 0] = high
        W[k, 1] = low
    pl.when(y == 0)(own_rows.wait)
    pl.when(src_l)(own_cols.wait)
    local[2].wait()

    @pl.when((core == 1) & (y != 0))
    def _():
        pl.semaphore_wait(answer, 1)

    def panel(side, q):
        cols = block(q)
        raw = U[side, :, cols]
        value = dot(W[side, 0], raw) + dot(W[side, 1], raw)
        UF[block(side), cols] = jnp.where((q > 0) | (c > 1), value, 0.0).astype(BF16)

        @pl.when((r == 0) & (side == 0) & ((q > 0) | (c > 0)))
        def _():
            M[0:NB, cols] = value.astype(BF16)

    def hand_on(side, g, first, tree):
        def event(j):
            j = j + first
            buf = u_part(U.at[side], j)
            remote(buf, buf, ur.at[side, j], ur.at[side, j], partner).wait_recv()
            for slot, cond, device in children[side][g]:
                pl.when(cond)(remote(buf, buf, us.at[side, g, slot], ur.at[side, j], device).start)

            @pl.when(lax.rem(j, 4) == 3)
            def _():
                q = j // 4
                raw = U.at[side, :, block(q)]
                remote(raw, raw, ps.at[side], pr.at[side, q], partner).start()
                if first >= 4 * SHARED:
                    panel(side, q)
                else:
                    pl.when(side != near_side)(lambda: panel(side, q))

        return event

    def take(side, q):
        @pl.when((y != 0) | (side == 1))
        def _():
            raw = U.at[side, :, block(q)]
            remote(raw, raw, pr.at[side, q], pr.at[side, q], partner).wait_recv()

        panel(side, q)

    def take_and_give(side, q):
        take(side, q)
        done = UF.at[block(side), block(q)]
        remote(done, done, fs.at[0], fr.at[0], partner).start()

    on_1 = []
    for side in range(2):
        for g, (tree, first, count, start, stride, arrival) in enumerate(GROUPS):
            at = lut(positions[side], arrival)
            if g == 0:
                at = jnp.where(c == 1 - side, lut(positions[side], FIRST[1]), at)
            on_1.append((start + at, stride, count, hand_on(side, g, first, tree)))

    def rows_of(j, base=0):
        return pl.ds(pl.multiple_of(base + j * LROWS, LROWS), LROWS)

    plane = []
    for slot in range(2):
        off = lut(z, offsets(FAR, slot))
        plane.append((hub & (off != 0), at_z(off)))
    plane.append((hub, at_x(-turn, 0)))
    plane_x = []
    for slot in range(3):
        off = lut(z, offsets(WIDE, slot))
        plane_x.append((off != 0, at_z(off)))

    def from_hub(side):
        return jnp.where(side == 0, x, lax.rem(1 - x + NX, NX))

    def column(j, slots):
        buf = L.at[rows_of(j)]

        @pl.when(jnp.logical_not(src_l))
        def _():
            remote(buf, buf, lr.at[j], lr.at[j], partner).wait_recv()

        for slot, (cond, device) in enumerate(plane):
            if slot in slots:
                pl.when(cond)(remote(buf, buf, ls.at[slot], lr.at[j], device).start)
        if 3 in slots:
            kept = L.at[rows_of(lax.rem(j, LCH // 2), 1024)]
            remote(buf, kept, ls.at[3], ll.at[0], at_x(turn, j // (LCH // 2))).start()

            @pl.when(jnp.logical_not(src_l) & (j >= LCH // 2))
            def _():
                remote(buf, buf, ls.at[4], lq.at[0], partner).start()

    def answered(place):
        @pl.when(hub & (n_down > place))
        def _():
            pl.semaphore_wait(ready.at[place], 1)

    def columns():
        @pl.when(src_l)
        def _():
            pl.loop(0, LCH // 2)(lambda j: column(j, (2, 3)))
            theirs = L.at[pl.ds(512, 512)]
            remote(theirs, theirs, lq.at[0], lq.at[0], partner).wait_recv()
            pl.loop(LCH // 2, LCH)(lambda j: column(j, (2, 3)))
            for slot in range(2):
                answered(slot)
                pl.loop(0, LCH)(lambda j: column(j, (slot,)))

        @pl.when(jnp.logical_not(src_l))
        def _():
            for place in range(3):
                answered(place)
            pl.loop(0, LCH)(lambda j: column(j, (0, 1, 2, 3)))

    def corner(j):
        buf = X.at[hb, rows_of(j)]

        @pl.when(z == 0)
        def _():
            X[hb, rows_of(j)] = U[hb, rows_of(j), 0:NB]

        @pl.when(z != 0)
        def _():
            remote(buf, buf, xr.at[j], xr.at[j], partner).wait_recv()

        for slot, (cond, device) in enumerate(plane_x):
            pl.when(cond)(remote(buf, buf, xs.at[slot], xr.at[j], device).start)
        for slot, off in enumerate((2, 1, -1)):
            remote(buf, buf, xs.at[3 + slot], xl.at[hb], at_x(off, 0)).start()

    def lower_rows(which, base):
        @pl.when(which == 0)
        def _():
            for part in range(2):
                raw = L[pl.ds(pl.multiple_of(base + part * NB, NB), NB)]
                value = dot(raw, W[2, 0]) + dot(raw, W[2, 1])
                LF[part * NB : (part + 1) * NB, 0:NB] = jnp.where(part * 16 + r > 0, value, 0.0).astype(BF16)

        @pl.when(which == 1)
        def _():
            for part in range(2):
                raw = L[pl.ds(pl.multiple_of(base + part * NB, NB), NB)]
                D1[part * NB : (part + 1) * NB] = dot(raw, W[3, 0]) + dot(raw, W[3, 1])

    def lower():
        @pl.when((core == 1) & jnp.logical_not(src_l))
        def _():
            remote(L.at[mine], L.at[mine], lq.at[0], lq.at[0], partner).wait_recv()

        lower_rows(fb, core * 512)
        kept = L.at[pl.ds(1024, 512)]
        remote(kept, kept, ll.at[0], ll.at[0], partner).wait_recv()
        lower_rows(1 - fb, 1024)

    def corners():
        @pl.when(first_core)
        def _():
            for k in range(2):

                @pl.when(x != 1 - k)
                def _():
                    remote(X.at[k], X.at[k], xl.at[k], xl.at[k], partner).wait_recv()

            remote(X, X, xs.at[6], xq.at[0], partner).start()

        @pl.when(core == 1)
        def _():
            remote(X, X, xq.at[0], xq.at[0], partner).wait_recv()

        l10 = (dot(X[1], W[2, 0]) + dot(X[1], W[2, 1])).astype(BF16)
        u01 = (dot(W[0, 0], X[0]) + dot(W[0, 1], X[0])).astype(BF16)
        small[0] = (dot(W[1, 0], l10) + dot(W[1, 1], l10)).astype(BF16)
        small[1] = (dot(u01, W[3, 0]) + dot(u01, W[3, 1])).astype(BF16)
        small[2] = u01
        for part in range(2):
            rows = pl.ds(part * NB, NB)
            at = part * 16 + r
            lower0 = LF[rows, 0:NB]
            lower1 = D1[rows] - dot(lower0, small[1])
            lower1 = jnp.where(at > 1, lower1, 0.0).astype(BF16)

            @pl.when((c == 0) & (at > 0))
            def _():
                M[rows, 0:NB] = lower0

            @pl.when((c == 1) & (at > 1))
            def _():
                M[rows, 0:NB] = lower1

            if part == 0:

                @pl.when((c == 1) & (r == 1))
                def _():
                    M[rows, 0:NB] = (M[rows, 0:NB].astype(F32) - dot(lower0, small[2])).astype(BF16)

            LF[rows, 0:NB] = (lower0.astype(F32) - dot(lower1, small[0])).astype(BF16)
            LF[rows, NB : 2 * NB] = lower1

    def steps(begin, end):
        @pl.loop(begin, end)
        def _(it):
            for start, stride, count, handle in on_1:
                k = it - start
                ok = (k >= 0) & (k < count * stride)
                if stride == 2:
                    ok = ok & (lax.rem(k, 2) == 0)

                @pl.when(ok)
                def _(k=k, stride=stride, handle=handle):
                    handle(k // stride if stride > 1 else k)

    @pl.when(first_core)
    def _():
        early = (y == 0) & (z != 0)
        had = jnp.where(src_l, hb, -1)

        def near_blocks():
            pl.loop(jnp.where(had == near_side, 1, 0), SHARED)(lambda q: take_and_give(near_side, q))

        def last_blocks():
            @pl.loop(SHARED, 7)
            def _(q):
                take(0, q)
                take(1, q)

        def far_blocks():
            middle = (y >= 3) & (y <= 5)
            pl.when(jnp.logical_not(middle))(last_blocks)
            pl.loop(jnp.where(had == 1 - near_side, 1, 0), SHARED)(lambda q: take(1 - near_side, q))
            pl.when(middle)(last_blocks)

        @pl.when(early)
        def _():
            near_blocks()
            far_blocks()

        columns()
        pl.when(had == near_side)(lambda: take_and_give(near_side, 0))
        pl.when(had == 1 - near_side)(lambda: take(1 - near_side, 0))

        @pl.when(hub)
        def _():
            pl.loop(0, XCH)(corner)

        lower()
        pl.when(jnp.logical_not(early))(near_blocks)
        corners()
        pl.when(jnp.logical_not(early))(far_blocks)

        for g, (tree, first, count, _, _, _) in enumerate(GROUPS):
            buf = U.at[0, :, pl.ds(first * 64, count * 64)]
            for slot, cond, device in children[0][g]:
                pl.when(cond & (y == 0))(remote(buf, buf, us.at[0, g, slot], ur.at[0, 0], device).wait_send)
        pl.when(y == 0)(remote(U.at[0], U.at[0], ps.at[0], pr.at[0, 0], partner).wait_send)
        shared = UF.at[0:NB, pl.ds(0, SHARED * NB)]
        remote(shared, shared, fs.at[0], fr.at[0], partner).wait_send()
        whole = L.at[pl.ds(0, 1024)]
        for slot, (cond, device) in enumerate(plane):
            pl.when(cond)(remote(whole, whole, ls.at[slot], lr.at[0], device).wait_send)
        remote(whole, whole, ls.at[3], ll.at[0], partner).wait_send()
        part = L.at[pl.ds(512, 512)]
        pl.when(jnp.logical_not(src_l))(remote(part, part, ls.at[4], lq.at[0], partner).wait_send)

        @pl.when(hub)
        def _():
            for slot, (cond, device) in enumerate(plane_x):
                pl.when(cond)(remote(X.at[0], X.at[0], xs.at[slot], xr.at[0], device).wait_send)
            for slot in range(3):
                remote(X.at[0], X.at[0], xs.at[3 + slot], xl.at[0], partner).wait_send()

        remote(X, X, xs.at[6], xq.at[0], partner).wait_send()

    @pl.when(core == 1)
    def _():
        mine_1 = L.at[pl.ds(512, 512)]
        give = remote(mine_1, mine_1, ls.at[4], lq.at[0], partner)
        pl.when(src_l)(give.start)
        lower_at, corners_at = lut(y, LOWER_AT), lut(y, CORNERS_AT)

        @pl.when(y == 0)
        def _():
            @pl.loop(0, 7)
            def _(q):
                raw = U[1, :, block(q)]
                value = dot(W[1, 0], raw) + dot(W[1, 1], raw)
                B1[:, block(q)] = value

                UF[NB : 2 * NB, block(q)] = jnp.where((q > 0) | (c > 1), value, 0.0).astype(BF16)

            main_sent(1, y == 0)
            for g, cond in last_groups:

                @pl.when(cond)
                def _(g=g):
                    @pl.loop(GROUPS[g][1], GROUPS[g][1] + GROUPS[g][2])
                    def _(j):
                        there = u_part(U.at[1], j)
                        remote(u_part(mat, j), there, us.at[1, g, 2], ur.at[1, j], at_y(1, 1)).start()

            remote(U.at[0], U.at[0], pr.at[0, 0], pr.at[0, 0], partner).wait_recv()
            pl.loop(SHARED, 7)(lambda q: panel(0, q))

        pl.when(y != 0)(lambda: steps(0, lower_at))
        lower()
        pl.when(y != 0)(lambda: steps(lower_at, corners_at))
        corners()
        pl.when(y != 0)(lambda: steps(corners_at, STEPS))
        shared = UF.at[0:NB, pl.ds(0, SHARED * NB)]
        remote(shared, shared, fr.at[0], fr.at[0], partner).wait_recv()

        @pl.when(y == 0)
        def _():
            LF[0:NB] = jnp.zeros((NB, 2 * NB), BF16)

            @pl.loop(0, COLS // NB)
            def _(q):
                cols = block(q)

                @pl.when((q > 0) | (c > 1))
                def _():
                    M[0:NB, cols] = (B1[:, cols] - dot(small[0], UF[0:NB, cols])).astype(BF16)

        @pl.when(y == 0)
        def _():
            for g, cond in last_groups:
                buf = U.at[1, :, pl.ds(GROUPS[g][1] * 64, GROUPS[g][2] * 64)]
                pl.when(cond)(remote(buf, buf, us.at[1, g, 2], ur.at[1, 0], partner).wait_send)

        for side in range(2):
            main_sent(side, y != 0)
            sent = remote(U.at[side], U.at[side], ps.at[side], pr.at[side, 0], partner)
            if side == 1:
                sent.wait_send()
            else:
                pl.when(y != 0)(sent.wait_send)
        pl.when(src_l)(give.wait_send)


def update(UF, LF, M, out, O, sems):
    copies = []
    for q in range(COLS // NB):
        cols = pl.ds(q * NB, NB)
        O[:, cols] = (M[:, cols].astype(F32) - dot(LF[...], UF[:, cols])).astype(BF16)
        copies.append(pltpu.make_async_copy(O.at[:, cols], out.at[:, cols], sems.at[q]))
        copies[-1].start()
    for copy in copies:
        copy.wait()


def body(matrix, lower_inv, upper_inv):
    D = pltpu.SemaphoreType.DMA
    vmem = pl.BlockSpec(memory_space=pltpu.VMEM)
    hbm = pl.BlockSpec(memory_space=pltpu.HBM)
    UF, LF, M = pl.pallas_call(
        gather,
        out_shape=(
            jax.ShapeDtypeStruct((2 * NB, COLS), BF16),
            jax.ShapeDtypeStruct((512, 2 * NB), BF16),
            jax.ShapeDtypeStruct((512, COLS), BF16),
        ),
        in_specs=[hbm] * 3,
        out_specs=(vmem, vmem, vmem),
        scratch_shapes=[
            pltpu.VMEM((2, NB, COLS), BF16),
            pltpu.VMEM((2, NB, NB), BF16),
            pltpu.VMEM((1536, NB), BF16),
            pltpu.VMEM((2, 2, NB, NB), F32),
            pltpu.VMEM((4, 2, NB, NB), BF16),
            pltpu.VMEM((3, NB, NB), BF16),
            pltpu.VMEM((512, NB), F32),
            D((2, 3, 3)),
            D((2, UCH)),
            D((2,)),
            D((2, 7)),
            D((1,)),
            D((1,)),
            D((5,)),
            D((LCH,)),
            D((1,)),
            D((1,)),
            D((7,)),
            D((XCH,)),
            D((2,)),
            D((1,)),
            pltpu.VMEM((NB, COLS), F32),
            pltpu.SemaphoreType.REGULAR((3,)),
            pltpu.SemaphoreType.REGULAR,
            D((5,)),
        ],
        compiler_params=pltpu.CompilerParams(
            collective_id=0, has_side_effects=True, vmem_limit_bytes=32 * 2**20
        ),
    )(*(pltpu.with_memory_space_constraint(a, pltpu.HBM) for a in (matrix, lower_inv, upper_inv)))
    return pl.pallas_call(
        update,
        out_shape=jax.ShapeDtypeStruct(matrix.shape, matrix.dtype),
        in_specs=[vmem] * 3,
        out_specs=hbm,
        scratch_shapes=[pltpu.VMEM((512, COLS), BF16), D((COLS // NB,))],
        compiler_params=pltpu.CompilerParams(vmem_limit_bytes=16 * 2**20),
    )(UF, LF, M)


def solution(mesh):
    in_specs = (P("row", "col"), P(), P())
    return jax.shard_map(body, mesh=mesh, in_specs=in_specs, out_specs=P("row", "col"), check_vma=False)
```
